32 devices in a mesh: row: 8 (over z, y), col: 4 (over x, core).
Axes of the slice: x: 2, y: 2, z: 4, core: 2. Of those that a mesh axis runs over, the one named last changes fastest.
Arguments:
- matrix: bfloat16 [4096, 4096], P('row', 'col'), may hold values from 0 to 0.0048828125, as said below
- in_mask: int32 [16, 16], P('row', 'col'), may hold values from 0 to 1, as said below
- out_mask: int32 [16, 16], P('row', 'col'), may hold values from 0 to 1, as said below
Outputs:
- flow: float32 [4096, 4096], P('row', 'col')
The draws below stay inside these ranges and needn't reach their ends.
Inputs may be any that keep to these rules, and one draw needn't show every extreme that they name: `matrix`: every diagonal entry is positive; all other entries are zero or positive. `in_mask`: tiles on the diagonal are 1. The block of tiles of one device holds at most 6 ones, and some device's block holds exactly 6. `out_mask`: tiles on the diagonal are 1.
All inputs are finite; a program needn't handle non-finite values.
Results may differ from the reference program's by a relative error of at most 0.0003.
Values may be sent and summed in bfloat16 or wider, within the bound.
No kernel may reach another device: no remote copies, remote signals or barrier semaphores. Data moves between devices by JAX's collectives and lax.ppermute only.
A program may use at most 128 MiB of HBM per device.

```python
import jax
import jax.numpy as jnp
from jax import lax

TILE = 256
NT = 16
ROWS = 4096
N_ROW = 8
N_COL = 4


def draw_matrix(key, part):
    key = jax.random.fold_in(key, 11)
    key_keep = jax.random.fold_in(key, 1)
    key_value = jax.random.fold_in(key, 2)
    low = 0.05 / ROWS
    high = 20.0 / ROWS
    keep_bits = jax.random.randint(key_keep, (ROWS, ROWS), 0, 4)
    rows_index = jnp.arange(ROWS)[:, None]
    cols_index = jnp.arange(ROWS)[None, :]
    keep = (keep_bits < 2) | (rows_index == cols_index)
    values = jnp.exp(jax.random.uniform(key_value, (ROWS, ROWS), jnp.float32, jnp.log(low), jnp.log(high)))
    return jnp.where(keep, values, 0.0).astype(jnp.bfloat16)


def draw_in_mask(key, part):
    key = jax.random.fold_in(key, 23)
    block_rows = NT // N_ROW
    block_cols = NT // N_COL
    most = block_rows * block_cols * 3 // 4
    floor_count = min(block_rows, block_cols)
    row_level = jax.random.randint(jax.random.fold_in(key, 1), (N_ROW,), 1, most + 1)
    col_level = jax.random.randint(jax.random.fold_in(key, 2), (N_COL,), 1, most + 1)
    counts = jnp.clip(1 + row_level[:, None] * col_level[None, :] // most, floor_count, most)
    chosen_row = jax.random.randint(jax.random.fold_in(key, 3), (), 0, N_ROW)
    chosen_col = jax.random.randint(jax.random.fold_in(key, 4), (), 0, N_COL)
    forced = (jnp.arange(N_ROW)[:, None] == chosen_row) & (jnp.arange(N_COL)[None, :] == chosen_col)
    counts = jnp.where(forced, most, counts).astype(jnp.int32)
    flat_index = (jnp.arange(NT)[:, None] * NT + jnp.arange(NT)[None, :]).astype(jnp.int32)
    scores = jax.random.randint(jax.random.fold_in(key, 5), (NT, NT), 0, 4096) * (NT * NT) + flat_index
    diagonal = jnp.arange(NT)[:, None] == jnp.arange(NT)[None, :]
    scores = jnp.where(diagonal, flat_index - NT * NT, scores).astype(jnp.int32)
    blocks = scores.reshape(N_ROW, block_rows, N_COL, block_cols).transpose(0, 2, 1, 3).reshape(N_ROW, N_COL, block_rows * block_cols)
    ranks = jnp.argsort(jnp.argsort(blocks, axis=-1), axis=-1)
    keep = (ranks < counts[:, :, None]).astype(jnp.int32)
    return keep.reshape(N_ROW, N_COL, block_rows, block_cols).transpose(0, 2, 1, 3).reshape(NT, NT)


def draw_out_mask(key, part):
    key = jax.random.fold_in(key, 37)
    rolled = jax.random.randint(key, (NT, NT), 0, 2)
    diagonal = jnp.arange(NT)[:, None] == jnp.arange(NT)[None, :]
    return ((rolled == 1) | diagonal).astype(jnp.int32)


def setup_inputs(seed: int = 0) -> dict:
    streams_of = jax.random.split(jax.random.key(seed), 4)
    matrix = draw_matrix(jax.random.fold_in(streams_of[3], 71), 0)
    in_mask = draw_in_mask(jax.random.fold_in(streams_of[3], 71), 0)
    out_mask = draw_out_mask(jax.random.fold_in(streams_of[3], 71), 0)
    return {"matrix": matrix, "in_mask": in_mask, "out_mask": out_mask}


def expand_tiles(tile_flags):
    return jnp.repeat(jnp.repeat(tile_flags, TILE, axis=0), TILE, axis=1).astype(jnp.float32)


def reference(matrix, in_mask, out_mask):
    active = matrix.astype(jnp.float32) * expand_tiles(in_mask)
    product = jnp.dot(active, active, precision=lax.Precision.HIGHEST, preferred_element_type=jnp.float32)
    inflated = product * product * expand_tiles(out_mask)
    totals = jnp.sum(inflated, axis=0)
    return float(ROWS) * inflated / totals[None, :]
```

```python
import functools

import jax
import jax.numpy as jnp
from jax import lax
from jax.experimental import pallas as pl
from jax.experimental.pallas import tpu as pltpu
from jax.sharding import PartitionSpec as P

CODE_ROWS = 16
VMEM_LIMIT = 16 * 1024 * 1024


def cost(weight=1):
    return pl.CostEstimate(flops=weight << 29, bytes_accessed=0, transcendentals=0)


class Sizes:
    def __init__(self, matrix, in_mask, n_row, n_col):
        self.rows, self.cols = matrix.shape
        self.tr, self.tc = in_mask.shape
        self.tile = self.rows // self.tr
        self.cap = self.tr * self.tc * 3 // 4
        self.pay_rows = CODE_ROWS + self.cap * self.tile
        self.buf_rows = self.pay_rows + self.tile
        self.cut = CODE_ROWS + (self.cap + 1) // 2 * self.tile
        self.chunks = ((0, self.cut), (self.cut, self.pay_rows - self.cut))
        self.n_row, self.n_col = n_row, n_col


def ring_order(n_row):
    n_out = 4 if n_row % 4 == 0 else 2
    n_in = n_row // n_out
    ring = [(0, 0)]
    for o in range(n_out):
        inner = list(range(1, n_in))
        ring += [(o, i) for i in (inner if o % 2 == 0 else inner[::-1])]
    ring += [(o, 0) for o in range(n_out - 1, 0, -1)]
    return [o * n_in + i for o, i in ring]


def pick(values, index):
    out = jnp.int32(values[0])
    for i, value in enumerate(values[1:], 1):
        out = jnp.where(index == i, value, out)
    return out


def origin(sz, key):
    ring = ring_order(sz.n_row)
    rows = [ring[(ring.index(q) - key) % sz.n_row] for q in range(sz.n_row)]
    return pick(rows, lax.axis_index("row"))


def pack_kernel(sz, mask_ref, matrix_ref, whole_ref, *chunk_refs):
    flags = [
        (mask_ref[t // sz.tc, t % sz.tc] != 0).astype(jnp.int32) for t in range(sz.tr * sz.tc)
    ]
    before, count = [], jnp.int32(0)
    for flag in flags:
        before.append(count)
        count = count + flag
    code = jnp.int32(0)
    for t, flag in enumerate(flags):
        code = code + flag * (1 << t)
    codes = jnp.full((CODE_ROWS, sz.tile), code.astype(jnp.float32), jnp.float32)
    codes = codes.astype(jnp.bfloat16)
    whole_ref[0:CODE_ROWS, :] = codes
    chunk_refs[0][0:CODE_ROWS, :] = codes
    for s in range(sz.cap):
        which = jnp.int32(0)
        for t, flag in enumerate(flags):
            which = jnp.where((flag == 1) & (before[t] == s), t, which)
        row = pl.multiple_of(which // sz.tc * sz.tile, sz.tile)
        col = pl.multiple_of(which % sz.tc * sz.tile, sz.tile)
        values = matrix_ref[pl.ds(row, sz.tile), pl.ds(col, sz.tile)]
        at = CODE_ROWS + s * sz.tile
        whole_ref[at : at + sz.tile, :] = values
        for ref, (start, size) in zip(chunk_refs, sz.chunks):
            if start <= at < start + size:
                ref[at - start : at - start + sz.tile, :] = values


def pack(sz, matrix, in_mask):
    vmem = pl.BlockSpec(memory_space=pltpu.VMEM)
    sizes = [sz.pay_rows] + [size for _, size in sz.chunks]
    return pl.pallas_call(
        functools.partial(pack_kernel, sz),
        out_shape=[pltpu.VMEM((size, sz.tile), jnp.bfloat16) for size in sizes],
        in_specs=[pl.BlockSpec(memory_space=pltpu.SMEM), vmem],
        out_specs=[vmem] * len(sizes),
        compiler_params=pltpu.CompilerParams(vmem_limit_bytes=VMEM_LIMIT),
        name="pack_tiles",
    )(*(pltpu.with_memory_space_constraint(x, pltpu.HBM) for x in (in_mask, matrix)))


def slots_of(sz, code_block):
    code = jnp.max(code_block.astype(jnp.float32)).astype(jnp.int32)
    slots, count = [], jnp.int32(0)
    for t in range(sz.tr * sz.tc):
        flag = lax.rem(lax.shift_right_logical(code, jnp.int32(t)), jnp.int32(2))
        slots.append(jnp.where(flag == 1, count, sz.cap))
        count = count + flag
    return slots


def slot_rows(sz, slot):
    return pl.ds(pl.multiple_of(CODE_ROWS + slot * sz.tile, 16), sz.tile)


def expand_kernel(sz, n, *refs):
    pays, dense, (buf, sems) = refs[:n], refs[n : 2 * n], refs[2 * n :]
    copies = []
    for p in range(n):
        copy = pltpu.make_async_copy(pays[p], buf.at[p, pl.ds(0, sz.pay_rows)], sems.at[p])
        copy.start()
        copies.append(copy)
        buf[p, sz.pay_rows :, :] = jnp.zeros((sz.tile, sz.tile), jnp.bfloat16)
    for p in range(n):
        copies[p].wait()
        slots = slots_of(sz, buf[p, 0:CODE_ROWS, 0:128])
        for t in range(sz.tr * sz.tc):
            a, k = t // sz.tc, t % sz.tc
            dense[p][a * sz.tile : (a + 1) * sz.tile, k * sz.tile : (k + 1) * sz.tile] = buf[
                p, slot_rows(sz, slots[t]), :
            ]


def expand(sz, pays, weight=1):
    n = len(pays)
    return pl.pallas_call(
        functools.partial(expand_kernel, sz, n),
        out_shape=[jax.ShapeDtypeStruct((sz.rows, sz.cols), jnp.bfloat16)] * n,
        in_specs=[pl.BlockSpec(memory_space=pltpu.HBM)] * n,
        out_specs=[pl.BlockSpec(memory_space=pltpu.VMEM)] * n,
        scratch_shapes=[
            pltpu.VMEM((n, sz.buf_rows, sz.tile), jnp.bfloat16),
            pltpu.SemaphoreType.DMA((n,)),
        ],
        compiler_params=pltpu.CompilerParams(vmem_limit_bytes=2 * VMEM_LIMIT),
        cost_estimate=cost(weight),
        name="expand_tiles",
    )(*pays)


def load_right(sz, buf, slots, b):
    tiles = [buf[slot_rows(sz, slots[k * sz.tc + b]), :] for k in range(sz.tr)]
    return jnp.concatenate(tiles, axis=0)


def start_left(sz, dist, blocks, key, into, sem):
    row = origin(sz, key)
    per_block = sz.cols // sz.rows
    column = pl.multiple_of(lax.rem(row, per_block) * sz.rows, sz.rows)
    apart = (row // per_block) ^ lax.axis_index("col")
    for d, block in zip(dist, blocks):

        @pl.when(apart == d)
        def _():
            pltpu.make_async_copy(block.at[:, pl.ds(column, sz.rows)], into, sem).start()


def wait_left(sz, blocks, into, sem):
    pltpu.make_async_copy(blocks[0].at[:, pl.ds(0, sz.rows)], into, sem).wait()


def on_core(core):
    if core is None:
        return jnp.bool_(True)
    return lax.axis_index("col") % 2 == core


def product_kernel(sz, dist, keys, first, then, *refs):
    refs = list(refs)
    blocks = [refs.pop(0) for _ in dist]
    pays = [[refs.pop(0) for _ in sz.chunks] for _ in keys]
    before_ref = None if first else refs.pop(0)
    out_ref = refs.pop(0)
    then_ref = None if then is None else refs.pop(0)
    buf, left, sems = refs
    per_piece = len(sz.chunks) + 1

    def copies(p):
        return [
            pltpu.make_async_copy(
                pays[p][h], buf.at[p, pl.ds(*chunk)], sems.at[p * per_piece + 1 + h]
            )
            for h, chunk in enumerate(sz.chunks)
        ]

    def begin(p, key):
        start_left(sz, dist, blocks, key, left.at[p], sems.at[p * per_piece])
        for copy in copies(p):
            copy.start()

    def add(p):
        buf[p, sz.pay_rows :, :] = jnp.zeros((sz.tile, sz.tile), jnp.bfloat16)
        wait_left(sz, blocks, left.at[p], sems.at[p * per_piece])
        for copy in copies(p):
            copy.wait()
        slots = slots_of(sz, buf[p, 0:CODE_ROWS, 0:128])
        for b in range(sz.tc):
            cols = slice(b * sz.tile, (b + 1) * sz.tile)
            term = jnp.dot(
                left[p], load_right(sz, buf.at[p], slots, b), preferred_element_type=jnp.float32
            )
            if p:
                term = term + out_ref[:, cols]
            elif not first:
                term = term + before_ref[:, cols]
            out_ref[:, cols] = term

    for p, (key, core) in enumerate(keys):
        if core is None:
            begin(p, key)
        else:
            pl.when(on_core(core))(functools.partial(begin, p, key))
    if then is not None:
        start_left(sz, dist, blocks, then, then_ref, sems.at[len(keys) * per_piece])
    for p, (key, core) in enumerate(keys):
        if core is None:
            add(p)
        else:
            pl.when(on_core(core))(functools.partial(add, p))
    if then is not None:
        wait_left(sz, blocks, then_ref, sems.at[len(keys) * per_piece])


def product(sz, before, dist, blocks, pieces, keys, then=None):
    n = len(keys)
    first = before is None
    vmem = pl.BlockSpec(memory_space=pltpu.VMEM)
    chunks = [chunk for piece in pieces for chunk in piece]
    in_specs = [pl.BlockSpec(memory_space=pl.ANY)] * len(blocks)
    in_specs += [pl.BlockSpec(memory_space=pltpu.HBM)] * len(chunks)
    args = [*blocks, *chunks]
    if not first:
        in_specs.append(vmem)
        args.append(before)
    out_shape = [jax.ShapeDtypeStruct((sz.rows, sz.cols), jnp.float32)]
    if then is not None:
        out_shape.append(jax.ShapeDtypeStruct((sz.rows, sz.rows), jnp.bfloat16))
    return pl.pallas_call(
        functools.partial(product_kernel, sz, dist, keys, first, then),
        out_shape=out_shape,
        in_specs=in_specs,
        out_specs=[vmem] * len(out_shape),
        scratch_shapes=[
            pltpu.VMEM((n, sz.buf_rows, sz.tile), jnp.bfloat16),
            pltpu.VMEM((n, sz.rows, sz.rows), jnp.bfloat16),
            pltpu.SemaphoreType.DMA((n * (len(sz.chunks) + 1) + 1,)),
        ],
        compiler_params=pltpu.CompilerParams(vmem_limit_bytes=VMEM_LIMIT),
        cost_estimate=cost(),
        name="product",
    )(*args)


def keep_kernel(sz, out_mask_ref, keep_ref):
    for a in range(sz.tr):
        for b in range(sz.tc):
            rows, cols = slice(a * 8, (a + 1) * 8), slice(b * sz.tile, (b + 1) * sz.tile)
            kept = (out_mask_ref[a, b] != 0).astype(jnp.float32)
            keep_ref[rows, cols] = jnp.full((8, sz.tile), kept, jnp.float32)


def keep_rows(sz, out_mask):
    return pl.pallas_call(
        functools.partial(keep_kernel, sz),
        out_shape=jax.ShapeDtypeStruct((8 * sz.tr, sz.cols), jnp.float32),
        in_specs=[pl.BlockSpec(memory_space=pltpu.SMEM)],
        out_specs=pl.BlockSpec(memory_space=pltpu.VMEM),
        compiler_params=pltpu.CompilerParams(vmem_limit_bytes=VMEM_LIMIT),
        cost_estimate=cost(),
        name="keep_rows",
    )(out_mask)


def last_kernel(sz, core, keep_ref, left_ref, *refs):
    refs = list(refs)
    pays = [refs.pop(0) for _ in sz.chunks]
    before_ref = refs.pop(0)
    known_ref = refs.pop(0) if core else None
    out_ref, sums_ref, buf = refs
    here = lax.axis_index("col") % 2 == core

    @pl.when(here)
    def _():
        for ref, chunk in zip(pays, sz.chunks):
            buf[pl.ds(*chunk), :] = ref[...]
        buf[sz.pay_rows :, :] = jnp.zeros((sz.tile, sz.tile), jnp.bfloat16)
        slots = slots_of(sz, buf[0:CODE_ROWS, 0:128])
        for b in range(sz.tc):
            cols = slice(b * sz.tile, (b + 1) * sz.tile)
            block = before_ref[:, cols] + jnp.dot(
                left_ref[...], load_right(sz, buf, slots, b), preferred_element_type=jnp.float32
            )
            total = jnp.zeros((1, sz.tile), jnp.float32)
            for a in range(sz.tr):
                rows = slice(a * sz.tile, (a + 1) * sz.tile)
                part = block[rows]
                kept = keep_ref[a * 8 : a * 8 + 1, cols] != 0
                part = jnp.where(kept, part * part, jnp.zeros_like(part))
                out_ref[rows, cols] = part
                total = total + jnp.sum(part, axis=0, keepdims=True)
            sums_ref[:, cols] = total

    @pl.when(jnp.logical_not(here))
    def _():
        sums_ref[...] = jnp.zeros_like(sums_ref) if known_ref is None else known_ref[...]


def last_product(sz, core, before, left, piece, keep, known=None):
    vmem = pl.BlockSpec(memory_space=pltpu.VMEM)
    args = [keep, left, *piece, before] + ([] if known is None else [known])
    return pl.pallas_call(
        functools.partial(last_kernel, sz, core),
        out_shape=[
            jax.ShapeDtypeStruct((sz.rows, sz.cols), jnp.float32),
            jax.ShapeDtypeStruct((1, sz.cols), jnp.float32),
        ],
        in_specs=[vmem] * len(args),
        out_specs=[vmem] * 2,
        scratch_shapes=[pltpu.VMEM((sz.buf_rows, sz.tile), jnp.bfloat16)],
        compiler_params=pltpu.CompilerParams(vmem_limit_bytes=VMEM_LIMIT),
        cost_estimate=cost(),
        name="product_last",
    )(*args)


def scale_kernel(sz, steps, first_ref, second_ref, totals_ref, flow_ref, buf, sems):
    total_rows = float(sz.rows * sz.n_row)
    size = sz.rows // steps
    totals = totals_ref[...]
    copies = []
    for s in range(steps):
        rows = pl.ds(s * size, size)
        for core, ref in enumerate((first_ref, second_ref)):

            @pl.when(lax.axis_index("col") % 2 == core)
            def _():
                buf[rows, :] = total_rows * ref[rows, :] / totals

        copies.append(pltpu.make_async_copy(buf.at[rows], flow_ref.at[rows], sems.at[s]))
        copies[-1].start()
    for copy in copies:
        copy.wait()


def scale(sz, first, second, totals):
    vmem = pl.BlockSpec(memory_space=pltpu.VMEM)
    steps = 4
    return pl.pallas_call(
        functools.partial(scale_kernel, sz, steps),
        out_shape=jax.ShapeDtypeStruct((sz.rows, sz.cols), jnp.float32),
        in_specs=[vmem] * 3,
        out_specs=pl.BlockSpec(memory_space=pltpu.HBM),
        scratch_shapes=[
            pltpu.VMEM((sz.rows, sz.cols), jnp.float32),
            pltpu.SemaphoreType.DMA((steps,)),
        ],
        compiler_params=pltpu.CompilerParams(vmem_limit_bytes=VMEM_LIMIT),
        cost_estimate=cost(),
        name="scale",
    )(first, second, totals)


def column_sums(sz, sums):
    if sz.n_row % 2:
        return lax.psum(sums, "row")
    pair = sums + lax.ppermute(sums, "row", [(q, q ^ 1) for q in range(sz.n_row)])
    others = [
        lax.ppermute(pair, "row", [(q, (q + 2 * t) % sz.n_row) for q in range(sz.n_row)])
        for t in range(1, sz.n_row // 2)
    ]
    return functools.reduce(jnp.add, others, pair)


def after(values, *anchors):
    return lax.optimization_barrier((*values, *anchors))[: len(values)]


def per_device(n_row, n_col, matrix, in_mask, out_mask):
    sz = Sizes(matrix, in_mask, n_row, n_col)
    ring = ring_order(n_row)
    half = n_row // 2

    whole, *own = pack(sz, matrix, in_mask)

    def hop(chunk, way):
        pairs = [(ring[p], ring[(p + way) % n_row]) for p in range(n_row)]
        return lax.ppermute(chunk, "row", pairs)

    def last_hop(chunk, way, core):
        pairs = [
            (ring[p] * n_col + c, (ring[(p + way) % n_row] if c % 2 == core else ring[p]) * n_col + c)
            for p in range(n_row)
            for c in range(n_col)
        ]
        return lax.ppermute(chunk, ("row", "col"), pairs)

    def apart(value, far):
        return lax.ppermute(value, "col", [(q, q ^ far) for q in range(n_col)])

    lead = {1: 0, -1: 1}
    pieces = {0: list(own)}
    arrivals = [(step, h) for step in range(1, half + 1) for h in (0, 1)][:-1]

    def send(step, h, sources):
        key = {way: way * step if step < half else half for way in (1, -1)}
        for way, source in zip((1, -1), sources):
            pieces.setdefault(key[way], [None] * 2)[lead[way] ^ h] = hop(source, way)

    def arrived(step, h):
        return [pieces[way * step if step < half else half][lead[way] ^ h] for way in (1, -1)]

    for h in (0, 1):
        send(1, h, [own[lead[way] ^ h] for way in (1, -1)])
    far = n_col // 2
    blocks, dense = {0: whole, 1: apart(whole, 1)}, {}
    acc, more, gate = None, [], []
    for i, (step, h) in enumerate(arrivals[:-1]):
        here = after(arrived(step, h), *gate)
        if i + 3 < len(arrivals):
            send(step + 1, h, here)
        elif i + 2 < len(arrivals):
            final = list(here)
            first = [last_hop(chunk, way, 0) for chunk, way in zip(final, (1, -1))]
        gate = list(here)
        if i == 0:
            mine, near = after([blocks[0], blocks[1]], *here)
            (dense[0],) = expand(sz, [mine], 12)
            if far > 1:
                blocks[far] = apart(after([whole], blocks[1])[0], far)
            gate += [dense[0], near]
        if i == 1:
            (dense[1],) = expand(sz, after([blocks[1]], *here), 12)
            gate += [dense[1]]
        if i == 1 and far > 1:
            (blocks[far],) = after([blocks[far]], *here)
        if i == 3:
            bit = far
            while bit > 2:
                bit //= 2
                for d in [d for d in blocks if d != 1]:
                    blocks[d ^ bit] = apart(blocks[d], bit)
            for d in [d for d in blocks if d > 1]:
                blocks[d ^ 1] = apart(blocks[d], 1)
            rest = sorted(d for d in blocks if d > 1)
            if rest:
                dense.update(zip(rest, expand(sz, after([blocks[d] for d in rest], *here))))
        if i == 1:
            keep = keep_rows(sz, after([out_mask], *here)[0])
            gate.append(keep)
        keys = None
        if i == 3:
            keys = [(0, None), (1, 0), (-1, 0)]
        elif i == 4:
            keys = [(2, None), (-2, None), (1, 1), (-1, 1)]
        elif i > 4 and h == 1:
            keys = [(step, None), (-step, None)]
        if keys:
            dist = sorted(dense)
            then = half if keys[0][0] == half - 1 else None
            chunks = [list(pieces[key]) for key, _ in keys]
            (chunks[0][0],) = after([chunks[0][0]], *here)
            acc, *more = product(sz, acc, dist, [dense[d] for d in dist], chunks, keys, then)
            gate.append(acc)
        if i + 3 == len(arrivals):
            final = after(final, acc)
            second = [last_hop(chunk, way, 1) for chunk, way in zip(final, (1, -1))]
    (left,) = more
    mine, sums = last_product(sz, 0, acc, left, first, keep)
    other, sums = last_product(sz, 1, acc, left, second, keep, sums)
    return scale(sz, mine, other, column_sums(sz, sums))


def solution(mesh):
    placed = (P("row", "col"), P("row", "col"), P("row", "col"))
    return jax.shard_map(
        functools.partial(per_device, mesh.shape["row"], mesh.shape["col"]),
        mesh=mesh,
        in_specs=placed,
        out_specs=P("row", "col"),
        check_vma=False,
    )
```

```python
import functools

import jax
import jax.numpy as jnp
from jax import lax
from jax.experimental import pallas as pl
from jax.experimental.pallas import tpu as pltpu
from jax.sharding import PartitionSpec as P

CODE_ROWS = 16
VMEM_LIMIT = 16 * 1024 * 1024


def cost(weight=1):
    return pl.CostEstimate(flops=weight << 29, bytes_accessed=0, transcendentals=0)


class Sizes:
    def __init__(self, matrix, in_mask, n_row, n_col):
        self.rows, self.cols = matrix.shape
        self.tr, self.tc = in_mask.shape
        self.tile = self.rows // self.tr
        self.cap = self.tr * self.tc * 3 // 4
        self.pay_rows = CODE_ROWS + self.cap * self.tile
        self.buf_rows = self.pay_rows + self.tile
        self.cut = CODE_ROWS + (self.cap + 1) // 2 * self.tile
        self.chunks = ((0, self.cut), (self.cut, self.pay_rows - self.cut))
        self.n_row, self.n_col = n_row, n_col


def ring_order(n_row):
    n_out = 4 if n_row % 4 == 0 else 2
    n_in = n_row // n_out
    ring = [(0, 0)]
    for o in range(n_out):
        inner = list(range(1, n_in))
        ring += [(o, i) for i in (inner if o % 2 == 0 else inner[::-1])]
    ring += [(o, 0) for o in range(n_out - 1, 0, -1)]
    return [o * n_in + i for o, i in ring]


def pick(values, index):
    out = jnp.int32(values[0])
    for i, value in enumerate(values[1:], 1):
        out = jnp.where(index == i, value, out)
    return out


def origin(sz, key):
    ring = ring_order(sz.n_row)
    rows = [ring[(ring.index(q) - key) % sz.n_row] for q in range(sz.n_row)]
    return pick(rows, lax.axis_index("row"))


def pack_kernel(sz, mask_ref, matrix_ref, whole_ref, *chunk_refs):
    flags = [
        (mask_ref[t // sz.tc, t % sz.tc] != 0).astype(jnp.int32) for t in range(sz.tr * sz.tc)
    ]
    before, count = [], jnp.int32(0)
    for flag in flags:
        before.append(count)
        count = count + flag
    code = jnp.int32(0)
    for t, flag in enumerate(flags):
        code = code + flag * (1 << t)
    codes = jnp.full((CODE_ROWS, sz.tile), code.astype(jnp.float32), jnp.float32)
    codes = codes.astype(jnp.bfloat16)
    whole_ref[0:CODE_ROWS, :] = codes
    chunk_refs[0][0:CODE_ROWS, :] = codes
    for s in range(sz.cap):
        which = jnp.int32(0)
        for t, flag in enumerate(flags):
            which = jnp.where((flag == 1) & (before[t] == s), t, which)
        row = pl.multiple_of(which // sz.tc * sz.tile, sz.tile)
        col = pl.multiple_of(which % sz.tc * sz.tile, sz.tile)
        values = matrix_ref[pl.ds(row, sz.tile), pl.ds(col, sz.tile)]
        at = CODE_ROWS + s * sz.tile
        whole_ref[at : at + sz.tile, :] = values
        for ref, (start, size) in zip(chunk_refs, sz.chunks):
            if start <= at < start + size:
                ref[at - start : at - start + sz.tile, :] = values


def pack(sz, matrix, in_mask):
    vmem = pl.BlockSpec(memory_space=pltpu.VMEM)
    sizes = [sz.pay_rows] + [size for _, size in sz.chunks]
    return pl.pallas_call(
        functools.partial(pack_kernel, sz),
        out_shape=[pltpu.VMEM((size, sz.tile), jnp.bfloat16) for size in sizes],
        in_specs=[pl.BlockSpec(memory_space=pltpu.SMEM), vmem],
        out_specs=[vmem] * len(sizes),
        compiler_params=pltpu.CompilerParams(vmem_limit_bytes=VMEM_LIMIT),
        name="pack_tiles",
    )(*(pltpu.with_memory_space_constraint(x, pltpu.HBM) for x in (in_mask, matrix)))


def slots_of(sz, code_block):
    code = jnp.max(code_block.astype(jnp.float32)).astype(jnp.int32)
    slots, count = [], jnp.int32(0)
    for t in range(sz.tr * sz.tc):
        flag = lax.rem(lax.shift_right_logical(code, jnp.int32(t)), jnp.int32(2))
        slots.append(jnp.where(flag == 1, count, sz.cap))
        count = count + flag
    return slots


def slot_rows(sz, slot):
    return pl.ds(pl.multiple_of(CODE_ROWS + slot * sz.tile, 16), sz.tile)


def expand_kernel(sz, n, *refs):
    pays, dense, (buf, sems) = refs[:n], refs[n : 2 * n], refs[2 * n :]
    copies = []
    for p in range(n):
        copy = pltpu.make_async_copy(pays[p], buf.at[p, pl.ds(0, sz.pay_rows)], sems.at[p])
        copy.start()
        copies.append(copy)
        buf[p, sz.pay_rows :, :] = jnp.zeros((sz.tile, sz.tile), jnp.bfloat16)
    for p in range(n):
        copies[p].wait()
        slots = slots_of(sz, buf[p, 0:CODE_ROWS, 0:128])
        for t in range(sz.tr * sz.tc):
            a, k = t // sz.tc, t % sz.tc
            dense[p][a * sz.tile : (a + 1) * sz.tile, k * sz.tile : (k + 1) * sz.tile] = buf[
                p, slot_rows(sz, slots[t]), :
            ]


def expand(sz, pays, weight=1):
    n = len(pays)
    return pl.pallas_call(
        functools.partial(expand_kernel, sz, n),
        out_shape=[jax.ShapeDtypeStruct((sz.rows, sz.cols), jnp.bfloat16)] * n,
        in_specs=[pl.BlockSpec(memory_space=pltpu.HBM)] * n,
        out_specs=[pl.BlockSpec(memory_space=pltpu.VMEM)] * n,
        scratch_shapes=[
            pltpu.VMEM((n, sz.buf_rows, sz.tile), jnp.bfloat16),
            pltpu.SemaphoreType.DMA((n,)),
        ],
        compiler_params=pltpu.CompilerParams(vmem_limit_bytes=2 * VMEM_LIMIT),
        cost_estimate=cost(weight),
        name="expand_tiles",
    )(*pays)


def load_right(sz, buf, slots, b):
    tiles = [buf[slot_rows(sz, slots[k * sz.tc + b]), :] for k in range(sz.tr)]
    return jnp.concatenate(tiles, axis=0)


def start_left(sz, dist, blocks, key, into, sem):
    row = origin(sz, key)
    per_block = sz.cols // sz.rows
    column = pl.multiple_of(lax.rem(row, per_block) * sz.rows, sz.rows)
    apart = (row // per_block) ^ lax.axis_index("col")
    for d, block in zip(dist, blocks):

        @pl.when(apart == d)
        def _():
            pltpu.make_async_copy(block.at[:, pl.ds(column, sz.rows)], into, sem).start()


def wait_left(sz, blocks, into, sem):
    pltpu.make_async_copy(blocks[0].at[:, pl.ds(0, sz.rows)], into, sem).wait()


def on_core(core):
    if core is None:
        return jnp.bool_(True)
    return lax.axis_index("col") % 2 == core


def product_kernel(sz, dist, keys, first, then, *refs):
    refs = list(refs)
    blocks = [refs.pop(0) for _ in dist]
    pays = [[refs.pop(0) for _ in sz.chunks] for _ in keys]
    before_ref = None if first else refs.pop(0)
    out_ref = refs.pop(0)
    then_refs = [refs.pop(0) for _ in then]
    buf, left, sems = refs
    per_piece = len(sz.chunks) + 1

    def copies(p):
        return [
            pltpu.make_async_copy(
                pays[p][h], buf.at[p, pl.ds(*chunk)], sems.at[p * per_piece + 1 + h]
            )
            for h, chunk in enumerate(sz.chunks)
        ]

    def begin(p, key):
        start_left(sz, dist, blocks, key, left.at[p], sems.at[p * per_piece])
        for copy in copies(p):
            copy.start()

    def add(p):
        buf[p, sz.pay_rows :, :] = jnp.zeros((sz.tile, sz.tile), jnp.bfloat16)
        wait_left(sz, blocks, left.at[p], sems.at[p * per_piece])
        for copy in copies(p):
            copy.wait()
        slots = slots_of(sz, buf[p, 0:CODE_ROWS, 0:128])
        for b in range(sz.tc):
            cols = slice(b * sz.tile, (b + 1) * sz.tile)
            term = jnp.dot(
                left[p], load_right(sz, buf.at[p], slots, b), preferred_element_type=jnp.float32
            )
            if p:
                term = term + out_ref[:, cols]
            elif not first:
                term = term + before_ref[:, cols]
            out_ref[:, cols] = term

    for p, (key, core) in enumerate(keys):
        if core is None:
            begin(p, key)
        else:
            pl.when(on_core(core))(functools.partial(begin, p, key))
    for t, (key, ref) in enumerate(zip(then, then_refs)):
        start_left(sz, dist, blocks, key, ref, sems.at[len(keys) * per_piece + t])
    for p, (key, core) in enumerate(keys):
        if core is None:
            add(p)
        else:
            pl.when(on_core(core))(functools.partial(add, p))
    for t, ref in enumerate(then_refs):
        wait_left(sz, blocks, ref, sems.at[len(keys) * per_piece + t])


def product(sz, before, dist, blocks, pieces, keys, then=()):
    n = len(keys)
    first = before is None
    vmem = pl.BlockSpec(memory_space=pltpu.VMEM)
    chunks = [chunk for piece in pieces for chunk in piece]
    in_specs = [pl.BlockSpec(memory_space=pl.ANY)] * len(blocks)
    in_specs += [pl.BlockSpec(memory_space=pltpu.HBM)] * len(chunks)
    args = [*blocks, *chunks]
    if not first:
        in_specs.append(vmem)
        args.append(before)
    out_shape = [jax.ShapeDtypeStruct((sz.rows, sz.cols), jnp.float32)]
    out_shape += [jax.ShapeDtypeStruct((sz.rows, sz.rows), jnp.bfloat16)] * len(then)
    return pl.pallas_call(
        functools.partial(product_kernel, sz, dist, keys, first, then),
        out_shape=out_shape,
        in_specs=in_specs,
        out_specs=[vmem] * len(out_shape),
        scratch_shapes=[
            pltpu.VMEM((n, sz.buf_rows, sz.tile), jnp.bfloat16),
            pltpu.VMEM((n, sz.rows, sz.rows), jnp.bfloat16),
            pltpu.SemaphoreType.DMA((n * (len(sz.chunks) + 1) + max(1, len(then)),)),
        ],
        compiler_params=pltpu.CompilerParams(vmem_limit_bytes=VMEM_LIMIT),
        cost_estimate=cost(),
        name="product",
    )(*args)


def near_kernel(sz, n, *refs):
    refs = list(refs)
    lefts = [refs.pop(0) for _ in range(n)]
    pays = [[refs.pop(0) for _ in sz.chunks] for _ in range(n)]
    before_ref, out_ref, buf = refs
    slots = []
    for p in range(n):
        for ref, chunk in zip(pays[p], sz.chunks):
            buf[p, pl.ds(*chunk), :] = ref[...]
        buf[p, sz.pay_rows :, :] = jnp.zeros((sz.tile, sz.tile), jnp.bfloat16)
        slots.append(slots_of(sz, buf[p, 0:CODE_ROWS, 0:128]))
    for b in range(sz.tc):
        cols = slice(b * sz.tile, (b + 1) * sz.tile)
        total = before_ref[:, cols]
        for p in range(n):
            total = total + jnp.dot(
                lefts[p][...],
                load_right(sz, buf.at[p], slots[p], b),
                preferred_element_type=jnp.float32,
            )
        out_ref[:, cols] = total


def near_product(sz, before, lefts, pieces):
    n = len(pieces)
    args = [*lefts, *(chunk for piece in pieces for chunk in piece), before]
    vmem = pl.BlockSpec(memory_space=pltpu.VMEM)
    return pl.pallas_call(
        functools.partial(near_kernel, sz, n),
        out_shape=jax.ShapeDtypeStruct((sz.rows, sz.cols), jnp.float32),
        in_specs=[vmem] * len(args),
        out_specs=vmem,
        scratch_shapes=[pltpu.VMEM((n, sz.buf_rows, sz.tile), jnp.bfloat16)],
        compiler_params=pltpu.CompilerParams(vmem_limit_bytes=VMEM_LIMIT),
        cost_estimate=cost(),
        name="product_near",
    )(*args)


def keep_kernel(sz, out_mask_ref, keep_ref):
    for a in range(sz.tr):
        for b in range(sz.tc):
            rows, cols = slice(a * 8, (a + 1) * 8), slice(b * sz.tile, (b + 1) * sz.tile)
            kept = (out_mask_ref[a, b] != 0).astype(jnp.float32)
            keep_ref[rows, cols] = jnp.full((8, sz.tile), kept, jnp.float32)


def keep_rows(sz, out_mask):
    return pl.pallas_call(
        functools.partial(keep_kernel, sz),
        out_shape=jax.ShapeDtypeStruct((8 * sz.tr, sz.cols), jnp.float32),
        in_specs=[pl.BlockSpec(memory_space=pltpu.SMEM)],
        out_specs=pl.BlockSpec(memory_space=pltpu.VMEM),
        compiler_params=pltpu.CompilerParams(vmem_limit_bytes=VMEM_LIMIT),
        cost_estimate=cost(),
        name="keep_rows",
    )(out_mask)


def last_kernel(sz, core, keep_ref, left_ref, *refs):
    refs = list(refs)
    pays = [refs.pop(0) for _ in sz.chunks]
    before_ref = refs.pop(0)
    known_ref = refs.pop(0) if core else None
    out_ref, sums_ref, buf = refs
    here = lax.axis_index("col") % 2 == core

    @pl.when(here)
    def _():
        for ref, chunk in zip(pays, sz.chunks):
            buf[pl.ds(*chunk), :] = ref[...]
        buf[sz.pay_rows :, :] = jnp.zeros((sz.tile, sz.tile), jnp.bfloat16)
        slots = slots_of(sz, buf[0:CODE_ROWS, 0:128])
        for b in range(sz.tc):
            cols = slice(b * sz.tile, (b + 1) * sz.tile)
            block = before_ref[:, cols] + jnp.dot(
                left_ref[...], load_right(sz, buf, slots, b), preferred_element_type=jnp.float32
            )
            total = jnp.zeros((1, sz.tile), jnp.float32)
            for a in range(sz.tr):
                rows = slice(a * sz.tile, (a + 1) * sz.tile)
                part = block[rows]
                kept = keep_ref[a * 8 : a * 8 + 1, cols] != 0
                part = jnp.where(kept, part * part, jnp.zeros_like(part))
                out_ref[rows, cols] = part
                total = total + jnp.sum(part, axis=0, keepdims=True)
            sums_ref[:, cols] = total

    @pl.when(jnp.logical_not(here))
    def _():
        sums_ref[...] = jnp.zeros_like(sums_ref) if known_ref is None else known_ref[...]


def last_product(sz, core, before, left, piece, keep, known=None):
    vmem = pl.BlockSpec(memory_space=pltpu.VMEM)
    args = [keep, left, *piece, before] + ([] if known is None else [known])
    return pl.pallas_call(
        functools.partial(last_kernel, sz, core),
        out_shape=[
            jax.ShapeDtypeStruct((sz.rows, sz.cols), jnp.float32),
            jax.ShapeDtypeStruct((1, sz.cols), jnp.float32),
        ],
        in_specs=[vmem] * len(args),
        out_specs=[vmem] * 2,
        scratch_shapes=[pltpu.VMEM((sz.buf_rows, sz.tile), jnp.bfloat16)],
        compiler_params=pltpu.CompilerParams(vmem_limit_bytes=VMEM_LIMIT),
        cost_estimate=cost(),
        name="product_last",
    )(*args)


def scale_kernel(sz, steps, first_ref, second_ref, totals_ref, flow_ref, buf, sems):
    total_rows = float(sz.rows * sz.n_row)
    size = sz.rows // steps
    share = 1.0 / totals_ref[...]
    copies = []
    for s in range(steps):
        rows = pl.ds(s * size, size)
        for core, ref in enumerate((first_ref, second_ref)):

            @pl.when(lax.axis_index("col") % 2 == core)
            def _():
                buf[rows, :] = (total_rows * ref[rows, :]) * share

        copies.append(pltpu.make_async_copy(buf.at[rows], flow_ref.at[rows], sems.at[s]))
        copies[-1].start()
    for copy in copies:
        copy.wait()


def scale(sz, first, second, totals):
    vmem = pl.BlockSpec(memory_space=pltpu.VMEM)
    steps = 4
    return pl.pallas_call(
        functools.partial(scale_kernel, sz, steps),
        out_shape=jax.ShapeDtypeStruct((sz.rows, sz.cols), jnp.float32),
        in_specs=[vmem] * 3,
        out_specs=pl.BlockSpec(memory_space=pltpu.HBM),
        scratch_shapes=[
            pltpu.VMEM((sz.rows, sz.cols), jnp.float32),
            pltpu.SemaphoreType.DMA((steps,)),
        ],
        compiler_params=pltpu.CompilerParams(vmem_limit_bytes=VMEM_LIMIT),
        cost_estimate=cost(),
        name="scale",
    )(first, second, totals)


def column_sums(sz, sums):
    if sz.n_row % 2:
        return lax.psum(sums, "row")
    pair = sums + lax.ppermute(sums, "row", [(q, q ^ 1) for q in range(sz.n_row)])
    others = [
        lax.ppermute(pair, "row", [(q, (q + 2 * t) % sz.n_row) for q in range(sz.n_row)])
        for t in range(1, sz.n_row // 2)
    ]
    return functools.reduce(jnp.add, others, pair)


def after(values, *anchors):
    return lax.optimization_barrier((*values, *anchors))[: len(values)]


def per_device(n_row, n_col, matrix, in_mask, out_mask):
    sz = Sizes(matrix, in_mask, n_row, n_col)
    ring = ring_order(n_row)
    half = n_row // 2

    whole, *own = pack(sz, matrix, in_mask)

    def hop(chunk, way):
        pairs = [(ring[p], ring[(p + way) % n_row]) for p in range(n_row)]
        return lax.ppermute(chunk, "row", pairs)

    def last_hop(chunk, way, core):
        pairs = [
            (ring[p] * n_col + c, (ring[(p + way) % n_row] if c % 2 == core else ring[p]) * n_col + c)
            for p in range(n_row)
            for c in range(n_col)
        ]
        return lax.ppermute(chunk, ("row", "col"), pairs)

    def apart(value, far):
        return lax.ppermute(value, "col", [(q, q ^ far) for q in range(n_col)])

    lead = {1: 0, -1: 1}
    pieces = {0: list(own)}
    arrivals = [(step, h) for step in range(1, half + 1) for h in (0, 1)][:-1]

    def send(step, h, sources):
        key = {way: way * step if step < half else half for way in (1, -1)}
        for way, source in zip((1, -1), sources):
            pieces.setdefault(key[way], [None] * 2)[lead[way] ^ h] = hop(source, way)

    def arrived(step, h):
        return [pieces[way * step if step < half else half][lead[way] ^ h] for way in (1, -1)]

    for h in (0, 1):
        send(1, h, [own[lead[way] ^ h] for way in (1, -1)])
    far = n_col // 2
    blocks, dense = {0: whole, 1: apart(whole, 1)}, {}
    acc, lefts, gate = None, [], []
    for i, (step, h) in enumerate(arrivals[:-1]):
        here = after(arrived(step, h), *gate)
        if i + 3 < len(arrivals):
            send(step + 1, h, here)
        elif i + 2 < len(arrivals):
            final = list(here)
            first = [last_hop(chunk, way, 0) for chunk, way in zip(final, (1, -1))]
        gate = list(here)
        if i == 0:
            mine, near = after([blocks[0], blocks[1]], *here)
            (dense[0],) = expand(sz, [mine], 12)
            if far > 1:
                blocks[far] = apart(after([whole], blocks[1])[0], far)
            gate += [dense[0], near]
        if i == 1:
            (dense[1],) = expand(sz, after([blocks[1]], *here), 12)
            gate += [dense[1]]
        if i == 1 and far > 1:
            (blocks[far],) = after([blocks[far]], *here)
        if i == 3:
            bit = far
            while bit > 2:
                bit //= 2
                for d in [d for d in blocks if d != 1]:
                    blocks[d ^ bit] = apart(blocks[d], bit)
            for d in [d for d in blocks if d > 1]:
                blocks[d ^ 1] = apart(blocks[d], 1)
            rest = sorted(d for d in blocks if d > 1)
            if rest:
                dense.update(zip(rest, expand(sz, after([blocks[d] for d in rest], *here))))
        if i == 1:
            keep = keep_rows(sz, after([out_mask], *here)[0])
            gate.append(keep)
        keys = None
        if i == 3:
            keys = [(0, None), (1, 0), (-1, 0)]
        elif i == 4:
            keys = [(2, None), (-2, None), (1, 1), (-1, 1)]
        elif i > 4 and h == 1:
            keys = [(step, None), (-step, None)]
        if keys:
            dist = sorted(dense)
            chunks = [list(pieces[key]) for key, _ in keys]
            (chunks[0][0],) = after([chunks[0][0]], *here)
            if keys[0][0] == half - 1:
                acc = near_product(sz, acc, lefts[:2], chunks)
            else:
                then = (half - 1, 1 - half, half) if keys[0][0] == half - 2 else ()
                acc, *lefts = product(sz, acc, dist, [dense[d] for d in dist], chunks, keys, then)
            gate.append(acc)
        if i + 3 == len(arrivals):
            final = after(final, acc)
            second = [last_hop(chunk, way, 1) for chunk, way in zip(final, (1, -1))]
    left = lefts[2]
    mine, sums = last_product(sz, 0, acc, left, first, keep)
    other, sums = last_product(sz, 1, acc, left, second, keep, sums)
    return scale(sz, mine, other, column_sums(sz, sums))


def solution(mesh):
    placed = (P("row", "col"), P("row", "col"), P("row", "col"))
    return jax.shard_map(
        functools.partial(per_device, mesh.shape["row"], mesh.shape["col"]),
        mesh=mesh,
        in_specs=placed,
        out_specs=P("row", "col"),
        check_vma=False,
    )
```

```python
import functools

import jax
import jax.numpy as jnp
from jax import lax
from jax.experimental import pallas as pl
from jax.experimental.pallas import tpu as pltpu
from jax.sharding import PartitionSpec as P

CODE_ROWS = 16
VMEM_LIMIT = 16 * 1024 * 1024


def cost(weight=1):
    return pl.CostEstimate(flops=weight << 29, bytes_accessed=0, transcendentals=0)


class Sizes:
    def __init__(self, matrix, in_mask, n_row, n_col):
        self.rows, self.cols = matrix.shape
        self.tr, self.tc = in_mask.shape
        self.tile = self.rows // self.tr
        self.cap = self.tr * self.tc * 3 // 4
        self.pay_rows = CODE_ROWS + self.cap * self.tile
        self.buf_rows = self.pay_rows + self.tile
        self.cut = CODE_ROWS + (self.cap + 1) // 2 * self.tile
        self.chunks = ((0, self.cut), (self.cut, self.pay_rows - self.cut))
        self.n_row, self.n_col = n_row, n_col


def ring_order(n_row):
    n_out = 4 if n_row % 4 == 0 else 2
    n_in = n_row // n_out
    ring = [(0, 0)]
    for o in range(n_out):
        inner = list(range(1, n_in))
        ring += [(o, i) for i in (inner if o % 2 == 0 else inner[::-1])]
    ring += [(o, 0) for o in range(n_out - 1, 0, -1)]
    return [o * n_in + i for o, i in ring]


def pick(values, index):
    out = jnp.int32(values[0])
    for i, value in enumerate(values[1:], 1):
        out = jnp.where(index == i, value, out)
    return out


def origin(sz, key):
    ring = ring_order(sz.n_row)
    rows = [ring[(ring.index(q) - key) % sz.n_row] for q in range(sz.n_row)]
    return pick(rows, lax.axis_index("row"))


def pack_kernel(sz, mask_ref, matrix_ref, whole_ref, *chunk_refs):
    flags = [
        (mask_ref[t // sz.tc, t % sz.tc] != 0).astype(jnp.int32) for t in range(sz.tr * sz.tc)
    ]
    before, count = [], jnp.int32(0)
    for flag in flags:
        before.append(count)
        count = count + flag
    code = jnp.int32(0)
    for t, flag in enumerate(flags):
        code = code + flag * (1 << t)
    codes = jnp.full((CODE_ROWS, sz.tile), code.astype(jnp.float32), jnp.float32)
    codes = codes.astype(jnp.bfloat16)
    whole_ref[0:CODE_ROWS, :] = codes
    chunk_refs[0][0:CODE_ROWS, :] = codes
    for s in range(sz.cap):
        which = jnp.int32(0)
        for t, flag in enumerate(flags):
            which = jnp.where((flag == 1) & (before[t] == s), t, which)
        row = pl.multiple_of(which // sz.tc * sz.tile, sz.tile)
        col = pl.multiple_of(which % sz.tc * sz.tile, sz.tile)
        values = matrix_ref[pl.ds(row, sz.tile), pl.ds(col, sz.tile)]
        at = CODE_ROWS + s * sz.tile
        whole_ref[at : at + sz.tile, :] = values
        for ref, (start, size) in zip(chunk_refs, sz.chunks):
            if start <= at < start + size:
                ref[at - start : at - start + sz.tile, :] = values


def pack(sz, matrix, in_mask):
    vmem = pl.BlockSpec(memory_space=pltpu.VMEM)
    sizes = [sz.pay_rows] + [size for _, size in sz.chunks]
    return pl.pallas_call(
        functools.partial(pack_kernel, sz),
        out_shape=[pltpu.VMEM((size, sz.tile), jnp.bfloat16) for size in sizes],
        in_specs=[pl.BlockSpec(memory_space=pltpu.SMEM), vmem],
        out_specs=[vmem] * len(sizes),
        compiler_params=pltpu.CompilerParams(vmem_limit_bytes=VMEM_LIMIT),
        name="pack_tiles",
    )(*(pltpu.with_memory_space_constraint(x, pltpu.HBM) for x in (in_mask, matrix)))


def slots_of(sz, code_block):
    code = jnp.max(code_block.astype(jnp.float32)).astype(jnp.int32)
    slots, count = [], jnp.int32(0)
    for t in range(sz.tr * sz.tc):
        flag = lax.rem(lax.shift_right_logical(code, jnp.int32(t)), jnp.int32(2))
        slots.append(jnp.where(flag == 1, count, sz.cap))
        count = count + flag
    return slots


def slot_rows(sz, slot):
    return pl.ds(pl.multiple_of(CODE_ROWS + slot * sz.tile, 16), sz.tile)


def expand_kernel(sz, n, *refs):
    pays, dense, (buf, sems) = refs[:n], refs[n : 2 * n], refs[2 * n :]
    copies = []
    for p in range(n):
        copy = pltpu.make_async_copy(pays[p], buf.at[p, pl.ds(0, sz.pay_rows)], sems.at[p])
        copy.start()
        copies.append(copy)
        buf[p, sz.pay_rows :, :] = jnp.zeros((sz.tile, sz.tile), jnp.bfloat16)
    for p in range(n):
        copies[p].wait()
        slots = slots_of(sz, buf[p, 0:CODE_ROWS, 0:128])
        for t in range(sz.tr * sz.tc):
            a, k = t // sz.tc, t % sz.tc
            dense[p][a * sz.tile : (a + 1) * sz.tile, k * sz.tile : (k + 1) * sz.tile] = buf[
                p, slot_rows(sz, slots[t]), :
            ]


def expand(sz, pays, weight=1):
    n = len(pays)
    return pl.pallas_call(
        functools.partial(expand_kernel, sz, n),
        out_shape=[jax.ShapeDtypeStruct((sz.rows, sz.cols), jnp.bfloat16)] * n,
        in_specs=[pl.BlockSpec(memory_space=pltpu.HBM)] * n,
        out_specs=[pl.BlockSpec(memory_space=pltpu.VMEM)] * n,
        scratch_shapes=[
            pltpu.VMEM((n, sz.buf_rows, sz.tile), jnp.bfloat16),
            pltpu.SemaphoreType.DMA((n,)),
        ],
        compiler_params=pltpu.CompilerParams(vmem_limit_bytes=2 * VMEM_LIMIT),
        cost_estimate=cost(weight),
        name="expand_tiles",
    )(*pays)


def load_right(sz, buf, slots, b):
    tiles = [buf[slot_rows(sz, slots[k * sz.tc + b]), :] for k in range(sz.tr)]
    return jnp.concatenate(tiles, axis=0)


def start_left(sz, dist, blocks, key, into, sem):
    row = origin(sz, key)
    per_block = sz.cols // sz.rows
    column = pl.multiple_of(lax.rem(row, per_block) * sz.rows, sz.rows)
    apart = (row // per_block) ^ lax.axis_index("col")
    for d, block in zip(dist, blocks):

        @pl.when(apart == d)
        def _():
            pltpu.make_async_copy(block.at[:, pl.ds(column, sz.rows)], into, sem).start()


def wait_left(sz, blocks, into, sem):
    pltpu.make_async_copy(blocks[0].at[:, pl.ds(0, sz.rows)], into, sem).wait()


def on_core(core):
    if core is None:
        return jnp.bool_(True)
    return lax.axis_index("col") % 2 == core


def product_kernel(sz, dist, keys, first, then, *refs):
    refs = list(refs)
    blocks = [refs.pop(0) for _ in dist]
    pays = [[refs.pop(0) for _ in sz.chunks] for _ in keys]
    before_ref = None if first else refs.pop(0)
    out_ref = refs.pop(0)
    then_refs = [refs.pop(0) for _ in then]
    buf, left, sems = refs
    per_piece = len(sz.chunks) + 1

    def copies(p):
        return [
            pltpu.make_async_copy(
                pays[p][h], buf.at[p, pl.ds(*chunk)], sems.at[p * per_piece + 1 + h]
            )
            for h, chunk in enumerate(sz.chunks)
        ]

    def begin(p, key):
        start_left(sz, dist, blocks, key, left.at[p], sems.at[p * per_piece])
        for copy in copies(p):
            copy.start()

    def add(p):
        buf[p, sz.pay_rows :, :] = jnp.zeros((sz.tile, sz.tile), jnp.bfloat16)
        wait_left(sz, blocks, left.at[p], sems.at[p * per_piece])
        for copy in copies(p):
            copy.wait()
        slots = slots_of(sz, buf[p, 0:CODE_ROWS, 0:128])
        for b in range(sz.tc):
            cols = slice(b * sz.tile, (b + 1) * sz.tile)
            term = jnp.dot(
                left[p], load_right(sz, buf.at[p], slots, b), preferred_element_type=jnp.float32
            )
            if p:
                term = term + out_ref[:, cols]
            elif not first:
                term = term + before_ref[:, cols]
            out_ref[:, cols] = term

    for p, (key, core) in enumerate(keys):
        if core is None:
            begin(p, key)
        else:
            pl.when(on_core(core))(functools.partial(begin, p, key))
    for t, (key, ref) in enumerate(zip(then, then_refs)):
        start_left(sz, dist, blocks, key, ref, sems.at[len(keys) * per_piece + t])
    for p, (key, core) in enumerate(keys):
        if core is None:
            add(p)
        else:
            pl.when(on_core(core))(functools.partial(add, p))
    for t, ref in enumerate(then_refs):
        wait_left(sz, blocks, ref, sems.at[len(keys) * per_piece + t])


def product(sz, before, dist, blocks, pieces, keys, then=()):
    n = len(keys)
    first = before is None
    vmem = pl.BlockSpec(memory_space=pltpu.VMEM)
    chunks = [chunk for piece in pieces for chunk in piece]
    in_specs = [pl.BlockSpec(memory_space=pl.ANY)] * len(blocks)
    in_specs += [pl.BlockSpec(memory_space=pltpu.HBM)] * len(chunks)
    args = [*blocks, *chunks]
    if not first:
        in_specs.append(vmem)
        args.append(before)
    out_shape = [jax.ShapeDtypeStruct((sz.rows, sz.cols), jnp.float32)]
    out_shape += [jax.ShapeDtypeStruct((sz.rows, sz.rows), jnp.bfloat16)] * len(then)
    return pl.pallas_call(
        functools.partial(product_kernel, sz, dist, keys, first, then),
        out_shape=out_shape,
        in_specs=in_specs,
        out_specs=[vmem] * len(out_shape),
        scratch_shapes=[
            pltpu.VMEM((n, sz.buf_rows, sz.tile), jnp.bfloat16),
            pltpu.VMEM((n, sz.rows, sz.rows), jnp.bfloat16),
            pltpu.SemaphoreType.DMA((n * (len(sz.chunks) + 1) + max(1, len(then)),)),
        ],
        compiler_params=pltpu.CompilerParams(vmem_limit_bytes=VMEM_LIMIT),
        cost_estimate=cost(),
        name="product",
    )(*args)


def near_kernel(sz, n, *refs):
    refs = list(refs)
    lefts = [refs.pop(0) for _ in range(n)]
    pays = [[refs.pop(0) for _ in sz.chunks] for _ in range(n)]
    before_ref, out_ref, buf = refs
    slots = []
    for p in range(n):
        for ref, chunk in zip(pays[p], sz.chunks):
            buf[p, pl.ds(*chunk), :] = ref[...]
        buf[p, sz.pay_rows :, :] = jnp.zeros((sz.tile, sz.tile), jnp.bfloat16)
        slots.append(slots_of(sz, buf[p, 0:CODE_ROWS, 0:128]))
    for b in range(sz.tc):
        cols = slice(b * sz.tile, (b + 1) * sz.tile)
        total = before_ref[:, cols]
        for p in range(n):
            total = total + jnp.dot(
                lefts[p][...],
                load_right(sz, buf.at[p], slots[p], b),
                preferred_element_type=jnp.float32,
            )
        out_ref[:, cols] = total


def near_product(sz, before, lefts, pieces):
    n = len(pieces)
    args = [*lefts, *(chunk for piece in pieces for chunk in piece), before]
    vmem = pl.BlockSpec(memory_space=pltpu.VMEM)
    return pl.pallas_call(
        functools.partial(near_kernel, sz, n),
        out_shape=jax.ShapeDtypeStruct((sz.rows, sz.cols), jnp.float32),
        in_specs=[vmem] * len(args),
        out_specs=vmem,
        scratch_shapes=[pltpu.VMEM((n, sz.buf_rows, sz.tile), jnp.bfloat16)],
        compiler_params=pltpu.CompilerParams(vmem_limit_bytes=VMEM_LIMIT),
        cost_estimate=cost(),
        name="product_near",
    )(*args)


def keep_kernel(sz, out_mask_ref, keep_ref):
    for a in range(sz.tr):
        for b in range(sz.tc):
            rows, cols = slice(a * 8, (a + 1) * 8), slice(b * sz.tile, (b + 1) * sz.tile)
            kept = (out_mask_ref[a, b] != 0).astype(jnp.float32)
            keep_ref[rows, cols] = jnp.full((8, sz.tile), kept, jnp.float32)


def keep_rows(sz, out_mask):
    return pl.pallas_call(
        functools.partial(keep_kernel, sz),
        out_shape=jax.ShapeDtypeStruct((8 * sz.tr, sz.cols), jnp.float32),
        in_specs=[pl.BlockSpec(memory_space=pltpu.SMEM)],
        out_specs=pl.BlockSpec(memory_space=pltpu.VMEM),
        compiler_params=pltpu.CompilerParams(vmem_limit_bytes=VMEM_LIMIT),
        cost_estimate=cost(),
        name="keep_rows",
    )(out_mask)


def last_kernel(sz, core, keep_ref, left_ref, *refs):
    refs = list(refs)
    pays = [refs.pop(0) for _ in sz.chunks]
    before_ref = refs.pop(0)
    known_ref = refs.pop(0) if core else None
    out_ref, sums_ref, buf = refs
    here = lax.axis_index("col") % 2 == core

    @pl.when(here)
    def _():
        for ref, chunk in zip(pays, sz.chunks):
            buf[pl.ds(*chunk), :] = ref[...]
        buf[sz.pay_rows :, :] = jnp.zeros((sz.tile, sz.tile), jnp.bfloat16)
        slots = slots_of(sz, buf[0:CODE_ROWS, 0:128])
        for b in range(sz.tc):
            cols = slice(b * sz.tile, (b + 1) * sz.tile)
            block = before_ref[:, cols] + jnp.dot(
                left_ref[...], load_right(sz, buf, slots, b), preferred_element_type=jnp.float32
            )
            total = jnp.zeros((1, sz.tile), jnp.float32)
            for a in range(sz.tr):
                rows = slice(a * sz.tile, (a + 1) * sz.tile)
                part = block[rows]
                kept = keep_ref[a * 8 : a * 8 + 1, cols] != 0
                part = jnp.where(kept, part * part, jnp.zeros_like(part))
                out_ref[rows, cols] = part
                total = total + jnp.sum(part, axis=0, keepdims=True)
            sums_ref[:, cols] = total

    @pl.when(jnp.logical_not(here))
    def _():
        sums_ref[...] = jnp.zeros_like(sums_ref) if known_ref is None else known_ref[...]


def last_product(sz, core, before, left, piece, keep, known=None):
    vmem = pl.BlockSpec(memory_space=pltpu.VMEM)
    args = [keep, left, *piece, before] + ([] if known is None else [known])
    return pl.pallas_call(
        functools.partial(last_kernel, sz, core),
        out_shape=[
            jax.ShapeDtypeStruct((sz.rows, sz.cols), jnp.float32),
            jax.ShapeDtypeStruct((1, sz.cols), jnp.float32),
        ],
        in_specs=[vmem] * len(args),
        out_specs=[vmem] * 2,
        scratch_shapes=[pltpu.VMEM((sz.buf_rows, sz.tile), jnp.bfloat16)],
        compiler_params=pltpu.CompilerParams(vmem_limit_bytes=VMEM_LIMIT),
        cost_estimate=cost(),
        name="product_last",
    )(*args)


def scale_kernel(sz, steps, first_ref, second_ref, totals_ref, flow_ref, buf, sems):
    total_rows = float(sz.rows * sz.n_row)
    size = sz.rows // steps
    totals = totals_ref[...]
    copies = []
    for s in range(steps):
        rows = pl.ds(s * size, size)
        for core, ref in enumerate((first_ref, second_ref)):

            @pl.when(lax.axis_index("col") % 2 == core)
            def _():
                buf[rows, :] = total_rows * ref[rows, :] / totals

        copies.append(pltpu.make_async_copy(buf.at[rows], flow_ref.at[rows], sems.at[s]))
        copies[-1].start()
    for copy in copies:
        copy.wait()


def scale(sz, first, second, totals):
    vmem = pl.BlockSpec(memory_space=pltpu.VMEM)
    steps = 4
    return pl.pallas_call(
        functools.partial(scale_kernel, sz, steps),
        out_shape=jax.ShapeDtypeStruct((sz.rows, sz.cols), jnp.float32),
        in_specs=[vmem] * 3,
        out_specs=pl.BlockSpec(memory_space=pltpu.HBM),
        scratch_shapes=[
            pltpu.VMEM((sz.rows, sz.cols), jnp.float32),
            pltpu.SemaphoreType.DMA((steps,)),
        ],
        compiler_params=pltpu.CompilerParams(vmem_limit_bytes=VMEM_LIMIT),
        cost_estimate=cost(),
        name="scale",
    )(first, second, totals)


def column_sums(sz, sums):
    if sz.n_row % 2:
        return lax.psum(sums, "row")
    pair = sums + lax.ppermute(sums, "row", [(q, q ^ 1) for q in range(sz.n_row)])
    others = [
        lax.ppermute(pair, "row", [(q, (q + 2 * t) % sz.n_row) for q in range(sz.n_row)])
        for t in range(1, sz.n_row // 2)
    ]
    return functools.reduce(jnp.add, others, pair)


def after(values, *anchors):
    return lax.optimization_barrier((*values, *anchors))[: len(values)]


def per_device(n_row, n_col, matrix, in_mask, out_mask):
    sz = Sizes(matrix, in_mask, n_row, n_col)
    ring = ring_order(n_row)
    half = n_row // 2

    whole, *own = pack(sz, matrix, in_mask)

    def hop(chunk, way):
        pairs = [(ring[p], ring[(p + way) % n_row]) for p in range(n_row)]
        return lax.ppermute(chunk, "row", pairs)

    def last_hop(chunk, way, core):
        pairs = [
            (ring[p] * n_col + c, (ring[(p + way) % n_row] if c % 2 == core else ring[p]) * n_col + c)
            for p in range(n_row)
            for c in range(n_col)
        ]
        return lax.ppermute(chunk, ("row", "col"), pairs)

    def apart(value, far):
        return lax.ppermute(value, "col", [(q, q ^ far) for q in range(n_col)])

    lead = {1: 0, -1: 1}
    pieces = {0: list(own)}
    arrivals = [(step, h) for step in range(1, half + 1) for h in (0, 1)][:-1]

    def send(step, h, sources):
        key = {way: way * step if step < half else half for way in (1, -1)}
        for way, source in zip((1, -1), sources):
            pieces.setdefault(key[way], [None] * 2)[lead[way] ^ h] = hop(source, way)

    def arrived(step, h):
        return [pieces[way * step if step < half else half][lead[way] ^ h] for way in (1, -1)]

    for h in (0, 1):
        send(1, h, [own[lead[way] ^ h] for way in (1, -1)])
    far = n_col // 2
    blocks, dense = {0: whole, 1: apart(whole, 1)}, {}
    acc, lefts, gate = None, [], []
    for i, (step, h) in enumerate(arrivals[:-1]):
        here = after(arrived(step, h), *gate)
        if i + 3 < len(arrivals):
            send(step + 1, h, here)
        elif i + 2 < len(arrivals):
            final = list(here)
            first = [last_hop(chunk, way, 0) for chunk, way in zip(final, (1, -1))]
        gate = list(here)
        if i == 0:
            mine, near = after([blocks[0], blocks[1]], *here)
            (dense[0],) = expand(sz, [mine], 12)
            if far > 1:
                blocks[far] = apart(after([whole], blocks[1])[0], far)
            gate += [dense[0], near]
        if i == 1:
            (dense[1],) = expand(sz, after([blocks[1]], *here), 12)
            gate += [dense[1]]
        if i == 1 and far > 1:
            (blocks[far],) = after([blocks[far]], *here)
        if i == 3:
            bit = far
            while bit > 2:
                bit //= 2
                for d in [d for d in blocks if d != 1]:
                    blocks[d ^ bit] = apart(blocks[d], bit)
            for d in [d for d in blocks if d > 1]:
                blocks[d ^ 1] = apart(blocks[d], 1)
            rest = sorted(d for d in blocks if d > 1)
            if rest:
                dense.update(zip(rest, expand(sz, after([blocks[d] for d in rest], *here))))
        if i == 1:
            keep = keep_rows(sz, after([out_mask], *here)[0])
            gate.append(keep)
        keys = None
        if i == 3:
            keys = [(0, None), (1, 0), (-1, 0)]
        elif i == 4:
            keys = [(2, None), (-2, None), (1, 1), (-1, 1)]
        elif i > 4 and h == 1:
            keys = [(step, None), (-step, None)]
        if keys:
            dist = sorted(dense)
            chunks = [list(pieces[key]) for key, _ in keys]
            (chunks[0][0],) = after([chunks[0][0]], *here)
            if keys[0][0] == half - 1:
                acc = near_product(sz, acc, lefts[:2], chunks)
            else:
                then = () if lefts else (half - 1, 1 - half, half)
                acc, *more = product(sz, acc, dist, [dense[d] for d in dist], chunks, keys, then)
                lefts = lefts or more
            gate.append(acc)
        if i + 3 == len(arrivals):
            final = after(final, acc)
            second = [last_hop(chunk, way, 1) for chunk, way in zip(final, (1, -1))]
    left = lefts[2]
    mine, sums = last_product(sz, 0, acc, left, first, keep)
    other, sums = last_product(sz, 1, acc, left, second, keep, sums)
    return scale(sz, mine, other, column_sums(sz, sums))


def solution(mesh):
    placed = (P("row", "col"), P("row", "col"), P("row", "col"))
    return jax.shard_map(
        functools.partial(per_device, mesh.shape["row"], mesh.shape["col"]),
        mesh=mesh,
        in_specs=placed,
        out_specs=P("row", "col"),
        check_vma=False,
    )
```

```python
import functools

import jax
import jax.numpy as jnp
from jax import lax
from jax.experimental import pallas as pl
from jax.experimental.pallas import tpu as pltpu
from jax.sharding import PartitionSpec as P

CODE_ROWS = 16
VMEM_LIMIT = 16 * 1024 * 1024


def cost(weight=1):
    return pl.CostEstimate(flops=weight << 29, bytes_accessed=0, transcendentals=0)


class Sizes:
    def __init__(self, matrix, in_mask, n_row, n_col):
        self.rows, self.cols = matrix.shape
        self.tr, self.tc = in_mask.shape
        self.tile = self.rows // self.tr
        self.cap = self.tr * self.tc * 3 // 4
        self.wide = min(self.tile, 128)
        self.parts = self.tile // self.wide
        self.slot = self.parts * self.tile
        self.pay_rows = CODE_ROWS + self.cap * self.slot
        self.buf_rows = self.pay_rows + self.slot
        self.cut = CODE_ROWS + (self.cap + 1) // 2 * self.slot
        self.chunks = ((0, self.cut), (self.cut, self.pay_rows - self.cut))
        self.n_row, self.n_col = n_row, n_col


def ring_order(n_row):
    n_out = 4 if n_row % 4 == 0 else 2
    n_in = n_row // n_out
    ring = [(0, 0)]
    for o in range(n_out):
        inner = list(range(1, n_in))
        ring += [(o, i) for i in (inner if o % 2 == 0 else inner[::-1])]
    ring += [(o, 0) for o in range(n_out - 1, 0, -1)]
    return [o * n_in + i for o, i in ring]


def pick(values, index):
    out = jnp.int32(values[0])
    for i, value in enumerate(values[1:], 1):
        out = jnp.where(index == i, value, out)
    return out


def origin(sz, key):
    ring = ring_order(sz.n_row)
    rows = [ring[(ring.index(q) - key) % sz.n_row] for q in range(sz.n_row)]
    return pick(rows, lax.axis_index("row"))


def pack_kernel(sz, mask_ref, matrix_ref, whole_ref, *chunk_refs):
    flags = [
        (mask_ref[t // sz.tc, t % sz.tc] != 0).astype(jnp.int32) for t in range(sz.tr * sz.tc)
    ]
    before, count = [], jnp.int32(0)
    for flag in flags:
        before.append(count)
        count = count + flag
    code = jnp.int32(0)
    for t, flag in enumerate(flags):
        code = code + flag * (1 << t)
    codes = jnp.full((CODE_ROWS, sz.wide), code.astype(jnp.float32), jnp.float32)
    codes = codes.astype(jnp.bfloat16)
    whole_ref[0:CODE_ROWS, :] = codes
    chunk_refs[0][0:CODE_ROWS, :] = codes
    for s in range(sz.cap):
        which = jnp.int32(0)
        for t, flag in enumerate(flags):
            which = jnp.where((flag == 1) & (before[t] == s), t, which)
        row = pl.multiple_of(which // sz.tc * sz.tile, sz.tile)
        col = pl.multiple_of(which % sz.tc * sz.tile, sz.tile)
        values = matrix_ref[pl.ds(row, sz.tile), pl.ds(col, sz.tile)]
        for j in range(sz.parts):
            part = values[:, j * sz.wide : (j + 1) * sz.wide]
            at = CODE_ROWS + s * sz.slot + j * sz.tile
            whole_ref[at : at + sz.tile, :] = part
            for ref, (start, size) in zip(chunk_refs, sz.chunks):
                if start <= at < start + size:
                    ref[at - start : at - start + sz.tile, :] = part


def pack(sz, matrix, in_mask):
    vmem = pl.BlockSpec(memory_space=pltpu.VMEM)
    sizes = [sz.pay_rows] + [size for _, size in sz.chunks]
    return pl.pallas_call(
        functools.partial(pack_kernel, sz),
        out_shape=[pltpu.VMEM((size, sz.wide), jnp.bfloat16) for size in sizes],
        in_specs=[pl.BlockSpec(memory_space=pltpu.SMEM), vmem],
        out_specs=[vmem] * len(sizes),
        compiler_params=pltpu.CompilerParams(vmem_limit_bytes=VMEM_LIMIT),
        name="pack_tiles",
    )(*(pltpu.with_memory_space_constraint(x, pltpu.HBM) for x in (in_mask, matrix)))


def slots_of(sz, code_block):
    code = jnp.max(code_block.astype(jnp.float32)).astype(jnp.int32)
    slots, count = [], jnp.int32(0)
    for t in range(sz.tr * sz.tc):
        flag = lax.rem(lax.shift_right_logical(code, jnp.int32(t)), jnp.int32(2))
        slots.append(jnp.where(flag == 1, count, sz.cap))
        count = count + flag
    return slots


def load_tile(sz, buf, slot):
    at = CODE_ROWS + slot * sz.slot
    parts = [
        buf[pl.ds(pl.multiple_of(at + j * sz.tile, 16), sz.tile), :] for j in range(sz.parts)
    ]
    return jnp.concatenate(parts, axis=1)


def clear_spare(sz, buf):
    buf[sz.pay_rows :, :] = jnp.zeros((sz.slot, sz.wide), jnp.bfloat16)


def expand_kernel(sz, n, *refs):
    pays, dense, (buf, sems) = refs[:n], refs[n : 2 * n], refs[2 * n :]
    copies = []
    for p in range(n):
        copy = pltpu.make_async_copy(pays[p], buf.at[p, pl.ds(0, sz.pay_rows)], sems.at[p])
        copy.start()
        copies.append(copy)
        clear_spare(sz, buf.at[p])
    for p in range(n):
        copies[p].wait()
        slots = slots_of(sz, buf[p, 0:CODE_ROWS, :])
        for t in range(sz.tr * sz.tc):
            a, k = t // sz.tc, t % sz.tc
            rows, cols = slice(a * sz.tile, (a + 1) * sz.tile), slice(k * sz.tile, (k + 1) * sz.tile)
            dense[p][rows, cols] = load_tile(sz, buf.at[p], slots[t])


def expand(sz, pays, weight=1):
    n = len(pays)
    return pl.pallas_call(
        functools.partial(expand_kernel, sz, n),
        out_shape=[jax.ShapeDtypeStruct((sz.rows, sz.cols), jnp.bfloat16)] * n,
        in_specs=[pl.BlockSpec(memory_space=pltpu.HBM)] * n,
        out_specs=[pl.BlockSpec(memory_space=pltpu.VMEM)] * n,
        scratch_shapes=[
            pltpu.VMEM((n, sz.buf_rows, sz.wide), jnp.bfloat16),
            pltpu.SemaphoreType.DMA((n,)),
        ],
        compiler_params=pltpu.CompilerParams(vmem_limit_bytes=2 * VMEM_LIMIT),
        cost_estimate=cost(weight),
        name="expand_tiles",
    )(*pays)


def load_right(sz, buf, slots, b):
    tiles = [load_tile(sz, buf, slots[k * sz.tc + b]) for k in range(sz.tr)]
    return jnp.concatenate(tiles, axis=0)


def start_left(sz, dist, blocks, key, into, sem):
    row = origin(sz, key)
    per_block = sz.cols // sz.rows
    column = pl.multiple_of(lax.rem(row, per_block) * sz.rows, sz.rows)
    apart = (row // per_block) ^ lax.axis_index("col")
    for d, block in zip(dist, blocks):

        @pl.when(apart == d)
        def _():
            pltpu.make_async_copy(block.at[:, pl.ds(column, sz.rows)], into, sem).start()


def wait_left(sz, blocks, into, sem):
    pltpu.make_async_copy(blocks[0].at[:, pl.ds(0, sz.rows)], into, sem).wait()


def on_core(core):
    if core is None:
        return jnp.bool_(True)
    return lax.axis_index("col") % 2 == core


def product_kernel(sz, dist, keys, first, then, *refs):
    refs = list(refs)
    blocks = [refs.pop(0) for _ in dist]
    pays = [[refs.pop(0) for _ in sz.chunks] for _ in keys]
    before_ref = None if first else refs.pop(0)
    out_ref = refs.pop(0)
    then_refs = [refs.pop(0) for _ in then]
    buf, left, sems = refs
    per_piece = len(sz.chunks) + 1

    def copies(p):
        return [
            pltpu.make_async_copy(
                pays[p][h], buf.at[p, pl.ds(*chunk)], sems.at[p * per_piece + 1 + h]
            )
            for h, chunk in enumerate(sz.chunks)
        ]

    def begin(p, key):
        start_left(sz, dist, blocks, key, left.at[p], sems.at[p * per_piece])
        for copy in copies(p):
            copy.start()

    def add(p):
        clear_spare(sz, buf.at[p])
        wait_left(sz, blocks, left.at[p], sems.at[p * per_piece])
        for copy in copies(p):
            copy.wait()
        slots = slots_of(sz, buf[p, 0:CODE_ROWS, :])
        for b in range(sz.tc):
            cols = slice(b * sz.tile, (b + 1) * sz.tile)
            term = jnp.dot(
                left[p], load_right(sz, buf.at[p], slots, b), preferred_element_type=jnp.float32
            )
            if p:
                term = term + out_ref[:, cols]
            elif not first:
                term = term + before_ref[:, cols]
            out_ref[:, cols] = term

    for p, (key, core) in enumerate(keys):
        if core is None:
            begin(p, key)
        else:
            pl.when(on_core(core))(functools.partial(begin, p, key))
    for t, (key, ref) in enumerate(zip(then, then_refs)):
        start_left(sz, dist, blocks, key, ref, sems.at[len(keys) * per_piece + t])
    for p, (key, core) in enumerate(keys):
        if core is None:
            add(p)
        else:
            pl.when(on_core(core))(functools.partial(add, p))
    for t, ref in enumerate(then_refs):
        wait_left(sz, blocks, ref, sems.at[len(keys) * per_piece + t])


def product(sz, before, dist, blocks, pieces, keys, then=()):
    n = len(keys)
    first = before is None
    vmem = pl.BlockSpec(memory_space=pltpu.VMEM)
    chunks = [chunk for piece in pieces for chunk in piece]
    in_specs = [pl.BlockSpec(memory_space=pl.ANY)] * len(blocks)
    in_specs += [pl.BlockSpec(memory_space=pltpu.HBM)] * len(chunks)
    args = [*blocks, *chunks]
    if not first:
        in_specs.append(vmem)
        args.append(before)
    out_shape = [jax.ShapeDtypeStruct((sz.rows, sz.cols), jnp.float32)]
    out_shape += [jax.ShapeDtypeStruct((sz.rows, sz.rows), jnp.bfloat16)] * len(then)
    return pl.pallas_call(
        functools.partial(product_kernel, sz, dist, keys, first, then),
        out_shape=out_shape,
        in_specs=in_specs,
        out_specs=[vmem] * len(out_shape),
        scratch_shapes=[
            pltpu.VMEM((n, sz.buf_rows, sz.wide), jnp.bfloat16),
            pltpu.VMEM((n, sz.rows, sz.rows), jnp.bfloat16),
            pltpu.SemaphoreType.DMA((n * (len(sz.chunks) + 1) + max(1, len(then)),)),
        ],
        compiler_params=pltpu.CompilerParams(vmem_limit_bytes=VMEM_LIMIT),
        cost_estimate=cost(),
        name="product",
    )(*args)


def near_kernel(sz, n, *refs):
    refs = list(refs)
    lefts = [refs.pop(0) for _ in range(n)]
    pays = [[refs.pop(0) for _ in sz.chunks] for _ in range(n)]
    before_ref, out_ref, buf = refs
    slots = []
    for p in range(n):
        for ref, chunk in zip(pays[p], sz.chunks):
            buf[p, pl.ds(*chunk), :] = ref[...]
        clear_spare(sz, buf.at[p])
        slots.append(slots_of(sz, buf[p, 0:CODE_ROWS, :]))
    for b in range(sz.tc):
        cols = slice(b * sz.tile, (b + 1) * sz.tile)
        total = before_ref[:, cols]
        for p in range(n):
            total = total + jnp.dot(
                lefts[p][...],
                load_right(sz, buf.at[p], slots[p], b),
                preferred_element_type=jnp.float32,
            )
        out_ref[:, cols] = total


def near_product(sz, before, lefts, pieces):
    n = len(pieces)
    args = [*lefts, *(chunk for piece in pieces for chunk in piece), before]
    vmem = pl.BlockSpec(memory_space=pltpu.VMEM)
    return pl.pallas_call(
        functools.partial(near_kernel, sz, n),
        out_shape=jax.ShapeDtypeStruct((sz.rows, sz.cols), jnp.float32),
        in_specs=[vmem] * len(args),
        out_specs=vmem,
        scratch_shapes=[pltpu.VMEM((n, sz.buf_rows, sz.wide), jnp.bfloat16)],
        compiler_params=pltpu.CompilerParams(vmem_limit_bytes=VMEM_LIMIT),
        cost_estimate=cost(),
        name="product_near",
    )(*args)


def keep_kernel(sz, out_mask_ref, keep_ref):
    for a in range(sz.tr):
        for b in range(sz.tc):
            rows, cols = slice(a * 8, (a + 1) * 8), slice(b * sz.tile, (b + 1) * sz.tile)
            kept = (out_mask_ref[a, b] != 0).astype(jnp.float32)
            keep_ref[rows, cols] = jnp.full((8, sz.tile), kept, jnp.float32)


def keep_rows(sz, out_mask):
    return pl.pallas_call(
        functools.partial(keep_kernel, sz),
        out_shape=jax.ShapeDtypeStruct((8 * sz.tr, sz.cols), jnp.float32),
        in_specs=[pl.BlockSpec(memory_space=pltpu.SMEM)],
        out_specs=pl.BlockSpec(memory_space=pltpu.VMEM),
        compiler_params=pltpu.CompilerParams(vmem_limit_bytes=VMEM_LIMIT),
        cost_estimate=cost(),
        name="keep_rows",
    )(out_mask)


def last_kernel(sz, core, keep_ref, left_ref, *refs):
    refs = list(refs)
    pays = [refs.pop(0) for _ in sz.chunks]
    before_ref = refs.pop(0)
    known_ref = refs.pop(0) if core else None
    out_ref, sums_ref, buf = refs
    here = lax.axis_index("col") % 2 == core

    @pl.when(here)
    def _():
        for ref, chunk in zip(pays, sz.chunks):
            buf[pl.ds(*chunk), :] = ref[...]
        clear_spare(sz, buf)
        slots = slots_of(sz, buf[0:CODE_ROWS, :])
        for b in range(sz.tc):
            cols = slice(b * sz.tile, (b + 1) * sz.tile)
            block = before_ref[:, cols] + jnp.dot(
                left_ref[...], load_right(sz, buf, slots, b), preferred_element_type=jnp.float32
            )
            total = jnp.zeros((1, sz.tile), jnp.float32)
            for a in range(sz.tr):
                rows = slice(a * sz.tile, (a + 1) * sz.tile)
                part = block[rows]
                kept = keep_ref[a * 8 : a * 8 + 1, cols] != 0
                part = jnp.where(kept, part * part, jnp.zeros_like(part))
                out_ref[rows, cols] = part
                total = total + jnp.sum(part, axis=0, keepdims=True)
            sums_ref[:, cols] = total

    @pl.when(jnp.logical_not(here))
    def _():
        sums_ref[...] = jnp.zeros_like(sums_ref) if known_ref is None else known_ref[...]


def last_product(sz, core, before, left, piece, keep, known=None):
    vmem = pl.BlockSpec(memory_space=pltpu.VMEM)
    args = [keep, left, *piece, before] + ([] if known is None else [known])
    return pl.pallas_call(
        functools.partial(last_kernel, sz, core),
        out_shape=[
            jax.ShapeDtypeStruct((sz.rows, sz.cols), jnp.float32),
            jax.ShapeDtypeStruct((1, sz.cols), jnp.float32),
        ],
        in_specs=[vmem] * len(args),
        out_specs=[vmem] * 2,
        scratch_shapes=[pltpu.VMEM((sz.buf_rows, sz.wide), jnp.bfloat16)],
        compiler_params=pltpu.CompilerParams(vmem_limit_bytes=VMEM_LIMIT),
        cost_estimate=cost(),
        name="product_last",
    )(*args)


def scale_kernel(sz, steps, first_ref, second_ref, totals_ref, flow_ref, buf, sems):
    total_rows = float(sz.rows * sz.n_row)
    size = sz.rows // steps
    totals = totals_ref[...]
    copies = []
    for s in range(steps):
        rows = pl.ds(s * size, size)
        for core, ref in enumerate((first_ref, second_ref)):

            @pl.when(lax.axis_index("col") % 2 == core)
            def _():
                buf[rows, :] = total_rows * ref[rows, :] / totals

        copies.append(pltpu.make_async_copy(buf.at[rows], flow_ref.at[rows], sems.at[s]))
        copies[-1].start()
    for copy in copies:
        copy.wait()


def scale(sz, first, second, totals):
    vmem = pl.BlockSpec(memory_space=pltpu.VMEM)
    steps = 4
    return pl.pallas_call(
        functools.partial(scale_kernel, sz, steps),
        out_shape=jax.ShapeDtypeStruct((sz.rows, sz.cols), jnp.float32),
        in_specs=[vmem] * 3,
        out_specs=pl.BlockSpec(memory_space=pltpu.HBM),
        scratch_shapes=[
            pltpu.VMEM((sz.rows, sz.cols), jnp.float32),
            pltpu.SemaphoreType.DMA((steps,)),
        ],
        compiler_params=pltpu.CompilerParams(vmem_limit_bytes=VMEM_LIMIT),
        cost_estimate=cost(),
        name="scale",
    )(first, second, totals)


def column_sums(sz, sums):
    if sz.n_row % 2:
        return lax.psum(sums, "row")
    pair = sums + lax.ppermute(sums, "row", [(q, q ^ 1) for q in range(sz.n_row)])
    others = [
        lax.ppermute(pair, "row", [(q, (q + 2 * t) % sz.n_row) for q in range(sz.n_row)])
        for t in range(1, sz.n_row // 2)
    ]
    return functools.reduce(jnp.add, others, pair)


def after(values, *anchors):
    return lax.optimization_barrier((*values, *anchors))[: len(values)]


def per_device(n_row, n_col, matrix, in_mask, out_mask):
    sz = Sizes(matrix, in_mask, n_row, n_col)
    ring = ring_order(n_row)
    half = n_row // 2

    whole, *own = pack(sz, matrix, in_mask)

    def hop(chunk, way):
        pairs = [(ring[p], ring[(p + way) % n_row]) for p in range(n_row)]
        return lax.ppermute(chunk, "row", pairs)

    def last_hop(chunk, way, core):
        pairs = [
            (ring[p] * n_col + c, (ring[(p + way) % n_row] if c % 2 == core else ring[p]) * n_col + c)
            for p in range(n_row)
            for c in range(n_col)
        ]
        return lax.ppermute(chunk, ("row", "col"), pairs)

    def apart(value, far):
        return lax.ppermute(value, "col", [(q, q ^ far) for q in range(n_col)])

    lead = {1: 0, -1: 1}
    pieces = {0: list(own)}
    arrivals = [(step, h) for step in range(1, half + 1) for h in (0, 1)][:-1]

    def send(step, h, sources):
        key = {way: way * step if step < half else half for way in (1, -1)}
        for way, source in zip((1, -1), sources):
            pieces.setdefault(key[way], [None] * 2)[lead[way] ^ h] = hop(source, way)

    def arrived(step, h):
        return [pieces[way * step if step < half else half][lead[way] ^ h] for way in (1, -1)]

    for h in (0, 1):
        send(1, h, [own[lead[way] ^ h] for way in (1, -1)])
    far = n_col // 2
    blocks, dense = {0: whole, 1: apart(whole, 1)}, {}
    acc, lefts, gate = None, [], []
    for i, (step, h) in enumerate(arrivals[:-1]):
        here = after(arrived(step, h), *gate)
        if i + 3 < len(arrivals):
            send(step + 1, h, here)
        elif i + 2 < len(arrivals):
            final = list(here)
            first = [last_hop(chunk, way, 0) for chunk, way in zip(final, (1, -1))]
        gate = list(here)
        if i == 0:
            mine, near = after([blocks[0], blocks[1]], *here)
            (dense[0],) = expand(sz, [mine], 12)
            if far > 1:
                blocks[far] = apart(after([whole], blocks[1])[0], far)
            gate += [dense[0], near]
        if i == 1:
            (dense[1],) = expand(sz, after([blocks[1]], *here), 12)
            gate += [dense[1]]
        if i == 1 and far > 1:
            (blocks[far],) = after([blocks[far]], *here)
        if i == 3:
            bit = far
            while bit > 2:
                bit //= 2
                for d in [d for d in blocks if d != 1]:
                    blocks[d ^ bit] = apart(blocks[d], bit)
            for d in [d for d in blocks if d > 1]:
                blocks[d ^ 1] = apart(blocks[d], 1)
            rest = sorted(d for d in blocks if d > 1)
            if rest:
                dense.update(zip(rest, expand(sz, after([blocks[d] for d in rest], *here))))
        if i == 1:
            keep = keep_rows(sz, after([out_mask], *here)[0])
            gate.append(keep)
        keys = None
        if i == 3:
            keys = [(0, None), (1, 0), (-1, 0)]
        elif i == 4:
            keys = [(2, None), (-2, None), (1, 1), (-1, 1)]
        elif i > 4 and h == 1:
            keys = [(step, None), (-step, None)]
        if keys:
            dist = sorted(dense)
            chunks = [list(pieces[key]) for key, _ in keys]
            (chunks[0][0],) = after([chunks[0][0]], *here)
            if keys[0][0] == half - 1:
                acc = near_product(sz, acc, lefts[:2], chunks)
            else:
                then = () if lefts else (half - 1, 1 - half, half)
                acc, *more = product(sz, acc, dist, [dense[d] for d in dist], chunks, keys, then)
                lefts = lefts or more
            gate.append(acc)
        if i + 3 == len(arrivals):
            final = after(final, acc)
            second = [last_hop(chunk, way, 1) for chunk, way in zip(final, (1, -1))]
    left = lefts[2]
    mine, sums = last_product(sz, 0, acc, left, first, keep)
    other, sums = last_product(sz, 1, acc, left, second, keep, sums)
    return scale(sz, mine, other, column_sums(sz, sums))


def solution(mesh):
    placed = (P("row", "col"), P("row", "col"), P("row", "col"))
    return jax.shard_map(
        functools.partial(per_device, mesh.shape["row"], mesh.shape["col"]),
        mesh=mesh,
        in_specs=placed,
        out_specs=P("row", "col"),
        check_vma=False,
    )
```

```python
import functools

import jax
import jax.numpy as jnp
from jax import lax
from jax.experimental import pallas as pl
from jax.experimental.pallas import tpu as pltpu
from jax.sharding import PartitionSpec as P

CODE_ROWS = 16
VMEM_LIMIT = 16 * 1024 * 1024


def cost(weight=1):
    return pl.CostEstimate(flops=weight << 29, bytes_accessed=0, transcendentals=0)


class Sizes:
    def __init__(self, matrix, in_mask, n_row, n_col):
        self.rows, self.cols = matrix.shape
        self.tr, self.tc = in_mask.shape
        self.tile = self.rows // self.tr
        self.cap = self.tr * self.tc * 3 // 4
        self.wide = min(self.tile, 128)
        self.parts = self.tile // self.wide
        self.slot = self.parts * self.tile
        self.pay_rows = CODE_ROWS + self.cap * self.slot
        self.buf_rows = self.pay_rows + self.slot
        self.cut = CODE_ROWS + (self.cap + 1) // 2 * self.slot
        self.chunks = ((0, self.cut), (self.cut, self.pay_rows - self.cut))
        self.n_row, self.n_col = n_row, n_col


def ring_order(n_row):
    n_out = 4 if n_row % 4 == 0 else 2
    n_in = n_row // n_out
    ring = [(0, 0)]
    for o in range(n_out):
        inner = list(range(1, n_in))
        ring += [(o, i) for i in (inner if o % 2 == 0 else inner[::-1])]
    ring += [(o, 0) for o in range(n_out - 1, 0, -1)]
    return [o * n_in + i for o, i in ring]


def pick(values, index):
    out = jnp.int32(values[0])
    for i, value in enumerate(values[1:], 1):
        out = jnp.where(index == i, value, out)
    return out


def origin(sz, key):
    ring = ring_order(sz.n_row)
    rows = [ring[(ring.index(q) - key) % sz.n_row] for q in range(sz.n_row)]
    return pick(rows, lax.axis_index("row"))


def pack_kernel(sz, mask_ref, matrix_ref, whole_ref, *chunk_refs):
    flags = [
        (mask_ref[t // sz.tc, t % sz.tc] != 0).astype(jnp.int32) for t in range(sz.tr * sz.tc)
    ]
    before, count = [], jnp.int32(0)
    for flag in flags:
        before.append(count)
        count = count + flag
    code = jnp.int32(0)
    for t, flag in enumerate(flags):
        code = code + flag * (1 << t)
    codes = jnp.full((CODE_ROWS, sz.wide), code.astype(jnp.float32), jnp.float32)
    codes = codes.astype(jnp.bfloat16)
    whole_ref[0:CODE_ROWS, :] = codes
    chunk_refs[0][0:CODE_ROWS, :] = codes
    for s in range(sz.cap):
        which = jnp.int32(0)
        for t, flag in enumerate(flags):
            which = jnp.where((flag == 1) & (before[t] == s), t, which)
        row = pl.multiple_of(which // sz.tc * sz.tile, sz.tile)
        col = pl.multiple_of(which % sz.tc * sz.tile, sz.tile)
        values = matrix_ref[pl.ds(row, sz.tile), pl.ds(col, sz.tile)]
        for j in range(sz.parts):
            part = values[:, j * sz.wide : (j + 1) * sz.wide]
            at = CODE_ROWS + s * sz.slot + j * sz.tile
            whole_ref[at : at + sz.tile, :] = part
            for ref, (start, size) in zip(chunk_refs, sz.chunks):
                if start <= at < start + size:
                    ref[at - start : at - start + sz.tile, :] = part


def pack(sz, matrix, in_mask):
    vmem = pl.BlockSpec(memory_space=pltpu.VMEM)
    sizes = [sz.pay_rows] + [size for _, size in sz.chunks]
    return pl.pallas_call(
        functools.partial(pack_kernel, sz),
        out_shape=[pltpu.VMEM((size, sz.wide), jnp.bfloat16) for size in sizes],
        in_specs=[pl.BlockSpec(memory_space=pltpu.SMEM), vmem],
        out_specs=[vmem] * len(sizes),
        compiler_params=pltpu.CompilerParams(vmem_limit_bytes=VMEM_LIMIT),
        name="pack_tiles",
    )(*(pltpu.with_memory_space_constraint(x, pltpu.HBM) for x in (in_mask, matrix)))


def slots_of(sz, code_block):
    code = jnp.max(code_block.astype(jnp.float32)).astype(jnp.int32)
    slots, count = [], jnp.int32(0)
    for t in range(sz.tr * sz.tc):
        flag = lax.rem(lax.shift_right_logical(code, jnp.int32(t)), jnp.int32(2))
        slots.append(jnp.where(flag == 1, count, sz.cap))
        count = count + flag
    return slots


def load_tile(sz, buf, slot):
    at = CODE_ROWS + slot * sz.slot
    parts = [
        buf[pl.ds(pl.multiple_of(at + j * sz.tile, 16), sz.tile), :] for j in range(sz.parts)
    ]
    return jnp.concatenate(parts, axis=1)


def clear_spare(sz, buf):
    buf[sz.pay_rows :, :] = jnp.zeros((sz.slot, sz.wide), jnp.bfloat16)


def expand_kernel(sz, n, *refs):
    pays, dense, (buf, sems) = refs[:n], refs[n : 2 * n], refs[2 * n :]
    copies = []
    for p in range(n):
        copy = pltpu.make_async_copy(pays[p], buf.at[p, pl.ds(0, sz.pay_rows)], sems.at[p])
        copy.start()
        copies.append(copy)
        clear_spare(sz, buf.at[p])
    for p in range(n):
        copies[p].wait()
        slots = slots_of(sz, buf[p, 0:CODE_ROWS, :])
        for t in range(sz.tr * sz.tc):
            a, k = t // sz.tc, t % sz.tc
            rows, cols = slice(a * sz.tile, (a + 1) * sz.tile), slice(k * sz.tile, (k + 1) * sz.tile)
            dense[p][rows, cols] = load_tile(sz, buf.at[p], slots[t])


def expand(sz, pays, weight=1):
    n = len(pays)
    return pl.pallas_call(
        functools.partial(expand_kernel, sz, n),
        out_shape=[jax.ShapeDtypeStruct((sz.rows, sz.cols), jnp.bfloat16)] * n,
        in_specs=[pl.BlockSpec(memory_space=pltpu.HBM)] * n,
        out_specs=[pl.BlockSpec(memory_space=pltpu.VMEM)] * n,
        scratch_shapes=[
            pltpu.VMEM((n, sz.buf_rows, sz.wide), jnp.bfloat16),
            pltpu.SemaphoreType.DMA((n,)),
        ],
        compiler_params=pltpu.CompilerParams(vmem_limit_bytes=2 * VMEM_LIMIT),
        cost_estimate=cost(weight),
        name="expand_tiles",
    )(*pays)


def load_right(sz, buf, slots, b):
    tiles = [load_tile(sz, buf, slots[k * sz.tc + b]) for k in range(sz.tr)]
    return jnp.concatenate(tiles, axis=0)


def start_left(sz, dist, blocks, key, into, sem):
    row = origin(sz, key)
    per_block = sz.cols // sz.rows
    column = pl.multiple_of(lax.rem(row, per_block) * sz.rows, sz.rows)
    apart = (row // per_block) ^ lax.axis_index("col")
    for d, block in zip(dist, blocks):

        @pl.when(apart == d)
        def _():
            pltpu.make_async_copy(block.at[:, pl.ds(column, sz.rows)], into, sem).start()


def wait_left(sz, blocks, into, sem):
    pltpu.make_async_copy(blocks[0].at[:, pl.ds(0, sz.rows)], into, sem).wait()


def on_core(core):
    if core is None:
        return jnp.bool_(True)
    return lax.axis_index("col") % 2 == core


def product_kernel(sz, dist, keys, first, then, *refs):
    refs = list(refs)
    blocks = [refs.pop(0) for _ in dist]
    pays = [[refs.pop(0) for _ in sz.chunks] for _ in keys]
    before_ref = None if first else refs.pop(0)
    out_ref = refs.pop(0)
    then_refs = [refs.pop(0) for _ in then]
    buf, left, sems = refs
    per_piece = len(sz.chunks) + 1

    def copies(p):
        return [
            pltpu.make_async_copy(
                pays[p][h], buf.at[p, pl.ds(*chunk)], sems.at[p * per_piece + 1 + h]
            )
            for h, chunk in enumerate(sz.chunks)
        ]

    def begin(p, key):
        start_left(sz, dist, blocks, key, left.at[p], sems.at[p * per_piece])
        for copy in copies(p):
            copy.start()

    def add(p):
        clear_spare(sz, buf.at[p])
        wait_left(sz, blocks, left.at[p], sems.at[p * per_piece])
        for copy in copies(p):
            copy.wait()
        slots = slots_of(sz, buf[p, 0:CODE_ROWS, :])
        for b in range(sz.tc):
            cols = slice(b * sz.tile, (b + 1) * sz.tile)
            term = jnp.dot(
                left[p], load_right(sz, buf.at[p], slots, b), preferred_element_type=jnp.float32
            )
            if p:
                term = term + out_ref[:, cols]
            elif not first:
                term = term + before_ref[:, cols]
            out_ref[:, cols] = term

    for p, (key, core) in enumerate(keys):
        if core is None:
            begin(p, key)
        else:
            pl.when(on_core(core))(functools.partial(begin, p, key))
    for t, (key, ref) in enumerate(zip(then, then_refs)):
        start_left(sz, dist, blocks, key, ref, sems.at[len(keys) * per_piece + t])
    for p, (key, core) in enumerate(keys):
        if core is None:
            add(p)
        else:
            pl.when(on_core(core))(functools.partial(add, p))
    for t, ref in enumerate(then_refs):
        wait_left(sz, blocks, ref, sems.at[len(keys) * per_piece + t])


def product(sz, before, dist, blocks, pieces, keys, then=()):
    n = len(keys)
    first = before is None
    vmem = pl.BlockSpec(memory_space=pltpu.VMEM)
    chunks = [chunk for piece in pieces for chunk in piece]
    in_specs = [pl.BlockSpec(memory_space=pl.ANY)] * len(blocks)
    in_specs += [pl.BlockSpec(memory_space=pltpu.HBM)] * len(chunks)
    args = [*blocks, *chunks]
    if not first:
        in_specs.append(vmem)
        args.append(before)
    out_shape = [jax.ShapeDtypeStruct((sz.rows, sz.cols), jnp.float32)]
    out_shape += [jax.ShapeDtypeStruct((sz.rows, sz.rows), jnp.bfloat16)] * len(then)
    return pl.pallas_call(
        functools.partial(product_kernel, sz, dist, keys, first, then),
        out_shape=out_shape,
        in_specs=in_specs,
        out_specs=[vmem] * len(out_shape),
        scratch_shapes=[
            pltpu.VMEM((n, sz.buf_rows, sz.wide), jnp.bfloat16),
            pltpu.VMEM((n, sz.rows, sz.rows), jnp.bfloat16),
            pltpu.SemaphoreType.DMA((n * (len(sz.chunks) + 1) + max(1, len(then)),)),
        ],
        compiler_params=pltpu.CompilerParams(vmem_limit_bytes=VMEM_LIMIT),
        cost_estimate=cost(),
        name="product",
    )(*args)


def near_kernel(sz, n, *refs):
    refs = list(refs)
    lefts = [refs.pop(0) for _ in range(n)]
    pays = [[refs.pop(0) for _ in sz.chunks] for _ in range(n)]
    before_ref, out_ref, buf = refs
    slots = []
    for p in range(n):
        for ref, chunk in zip(pays[p], sz.chunks):
            buf[p, pl.ds(*chunk), :] = ref[...]
        clear_spare(sz, buf.at[p])
        slots.append(slots_of(sz, buf[p, 0:CODE_ROWS, :]))
    for b in range(sz.tc):
        cols = slice(b * sz.tile, (b + 1) * sz.tile)
        total = before_ref[:, cols]
        for p in range(n):
            total = total + jnp.dot(
                lefts[p][...],
                load_right(sz, buf.at[p], slots[p], b),
                preferred_element_type=jnp.float32,
            )
        out_ref[:, cols] = total


def near_product(sz, before, lefts, pieces):
    n = len(pieces)
    args = [*lefts, *(chunk for piece in pieces for chunk in piece), before]
    vmem = pl.BlockSpec(memory_space=pltpu.VMEM)
    return pl.pallas_call(
        functools.partial(near_kernel, sz, n),
        out_shape=jax.ShapeDtypeStruct((sz.rows, sz.cols), jnp.float32),
        in_specs=[vmem] * len(args),
        out_specs=vmem,
        scratch_shapes=[pltpu.VMEM((n, sz.buf_rows, sz.wide), jnp.bfloat16)],
        compiler_params=pltpu.CompilerParams(vmem_limit_bytes=VMEM_LIMIT),
        cost_estimate=cost(),
        name="product_near",
    )(*args)


def keep_kernel(sz, out_mask_ref, keep_ref):
    for a in range(sz.tr):
        for b in range(sz.tc):
            rows, cols = slice(a * 8, (a + 1) * 8), slice(b * sz.tile, (b + 1) * sz.tile)
            kept = (out_mask_ref[a, b] != 0).astype(jnp.float32)
            keep_ref[rows, cols] = jnp.full((8, sz.tile), kept, jnp.float32)


def keep_rows(sz, out_mask):
    return pl.pallas_call(
        functools.partial(keep_kernel, sz),
        out_shape=jax.ShapeDtypeStruct((8 * sz.tr, sz.cols), jnp.float32),
        in_specs=[pl.BlockSpec(memory_space=pltpu.SMEM)],
        out_specs=pl.BlockSpec(memory_space=pltpu.VMEM),
        compiler_params=pltpu.CompilerParams(vmem_limit_bytes=VMEM_LIMIT),
        cost_estimate=cost(),
        name="keep_rows",
    )(out_mask)


def last_kernel(sz, core, keep_ref, left_ref, *refs):
    refs = list(refs)
    pays = [refs.pop(0) for _ in sz.chunks]
    before_ref = refs.pop(0)
    known_ref = refs.pop(0) if core else None
    out_ref, sums_ref, buf = refs
    here = lax.axis_index("col") % 2 == core

    @pl.when(here)
    def _():
        for ref, chunk in zip(pays, sz.chunks):
            buf[pl.ds(*chunk), :] = ref[...]
        clear_spare(sz, buf)
        slots = slots_of(sz, buf[0:CODE_ROWS, :])
        for b in range(sz.tc):
            cols = slice(b * sz.tile, (b + 1) * sz.tile)
            block = before_ref[:, cols] + jnp.dot(
                left_ref[...], load_right(sz, buf, slots, b), preferred_element_type=jnp.float32
            )
            total = jnp.zeros((1, sz.tile), jnp.float32)
            for a in range(sz.tr):
                rows = slice(a * sz.tile, (a + 1) * sz.tile)
                part = block[rows]
                kept = keep_ref[a * 8 : a * 8 + 1, cols] != 0
                part = jnp.where(kept, part * part, jnp.zeros_like(part))
                out_ref[rows, cols] = part
                total = total + jnp.sum(part, axis=0, keepdims=True)
            sums_ref[:, cols] = total

    @pl.when(jnp.logical_not(here))
    def _():
        sums_ref[...] = jnp.zeros_like(sums_ref) if known_ref is None else known_ref[...]


def last_product(sz, core, before, left, piece, keep, known=None):
    vmem = pl.BlockSpec(memory_space=pltpu.VMEM)
    args = [keep, left, *piece, before] + ([] if known is None else [known])
    return pl.pallas_call(
        functools.partial(last_kernel, sz, core),
        out_shape=[
            jax.ShapeDtypeStruct((sz.rows, sz.cols), jnp.float32),
            jax.ShapeDtypeStruct((1, sz.cols), jnp.float32),
        ],
        in_specs=[vmem] * len(args),
        out_specs=[vmem] * 2,
        scratch_shapes=[pltpu.VMEM((sz.buf_rows, sz.wide), jnp.bfloat16)],
        compiler_params=pltpu.CompilerParams(vmem_limit_bytes=VMEM_LIMIT),
        cost_estimate=cost(),
        name="product_last",
    )(*args)


def scale_kernel(sz, steps, first_ref, second_ref, totals_ref, flow_ref, buf, sems):
    total_rows = float(sz.rows * sz.n_row)
    size = sz.rows // steps
    totals = totals_ref[...]
    copies = []
    for s in range(steps):
        rows = pl.ds(s * size, size)
        for core, ref in enumerate((first_ref, second_ref)):

            @pl.when(lax.axis_index("col") % 2 == core)
            def _():
                buf[rows, :] = total_rows * ref[rows, :] / totals

        copies.append(pltpu.make_async_copy(buf.at[rows], flow_ref.at[rows], sems.at[s]))
        copies[-1].start()
    for copy in copies:
        copy.wait()


def scale(sz, first, second, totals):
    vmem = pl.BlockSpec(memory_space=pltpu.VMEM)
    steps = 4
    return pl.pallas_call(
        functools.partial(scale_kernel, sz, steps),
        out_shape=jax.ShapeDtypeStruct((sz.rows, sz.cols), jnp.float32),
        in_specs=[vmem] * 3,
        out_specs=pl.BlockSpec(memory_space=pltpu.HBM),
        scratch_shapes=[
            pltpu.VMEM((sz.rows, sz.cols), jnp.float32),
            pltpu.SemaphoreType.DMA((steps,)),
        ],
        compiler_params=pltpu.CompilerParams(vmem_limit_bytes=VMEM_LIMIT),
        cost_estimate=cost(),
        name="scale",
    )(first, second, totals)


def column_sums(sz, sums):
    if sz.n_row % 2:
        return lax.psum(sums, "row")
    pair = sums + lax.ppermute(sums, "row", [(q, q ^ 1) for q in range(sz.n_row)])
    others = [
        lax.ppermute(pair, "row", [(q, (q + 2 * t) % sz.n_row) for q in range(sz.n_row)])
        for t in range(1, sz.n_row // 2)
    ]
    return functools.reduce(jnp.add, others, pair)


def after(values, *anchors):
    return lax.optimization_barrier((*values, *anchors))[: len(values)]


def per_device(n_row, n_col, matrix, in_mask, out_mask):
    sz = Sizes(matrix, in_mask, n_row, n_col)
    ring = ring_order(n_row)
    half = n_row // 2

    whole, *own = pack(sz, matrix, in_mask)

    def hop(chunk, way):
        pairs = [(ring[p], ring[(p + way) % n_row]) for p in range(n_row)]
        return lax.ppermute(chunk, "row", pairs)

    def last_hop(chunk, way, core, keep=False):
        aside = 2 if n_col % 4 == 0 and not keep else 0
        pairs = []
        for p in range(n_row):
            for c in range(n_col):
                mine = c % 2 == core
                to = (ring[(p + way) % n_row], c) if mine else (ring[p], c ^ aside)
                pairs.append((ring[p] * n_col + c, to[0] * n_col + to[1]))
        return lax.ppermute(chunk, ("row", "col"), pairs)

    def apart(value, far):
        return lax.ppermute(value, "col", [(q, q ^ far) for q in range(n_col)])

    lead = {1: 0, -1: 1}
    pieces = {0: list(own)}
    arrivals = [(step, h) for step in range(1, half + 1) for h in (0, 1)][:-1]

    def send(step, h, sources):
        key = {way: way * step if step < half else half for way in (1, -1)}
        for way, source in zip((1, -1), sources):
            pieces.setdefault(key[way], [None] * 2)[lead[way] ^ h] = hop(source, way)

    def arrived(step, h):
        return [pieces[way * step if step < half else half][lead[way] ^ h] for way in (1, -1)]

    for h in (0, 1):
        send(1, h, [own[lead[way] ^ h] for way in (1, -1)])
    far = n_col // 2
    blocks, dense = {0: whole, 1: apart(whole, 1)}, {}
    acc, lefts, gate = None, [], []
    for i, (step, h) in enumerate(arrivals[:-1]):
        here = after(arrived(step, h), *gate)
        if i + 3 < len(arrivals):
            send(step + 1, h, here)
        elif i + 2 < len(arrivals):
            final = list(here)
            first = [last_hop(chunk, way, 0) for chunk, way in zip(final, (1, -1))]
        gate = list(here)
        if i == 0:
            mine, near = after([blocks[0], blocks[1]], *here)
            (dense[0],) = expand(sz, [mine], 12)
            if far > 1:
                blocks[far] = apart(after([whole], blocks[1])[0], far)
            gate += [dense[0], near]
        if i == 1:
            (dense[1],) = expand(sz, after([blocks[1]], *here), 12)
            gate += [dense[1]]
        if i == 1 and far > 1:
            (blocks[far],) = after([blocks[far]], *here)
        if i == 3:
            bit = far
            while bit > 2:
                bit //= 2
                for d in [d for d in blocks if d != 1]:
                    blocks[d ^ bit] = apart(blocks[d], bit)
            for d in [d for d in blocks if d > 1]:
                blocks[d ^ 1] = apart(blocks[d], 1)
            rest = sorted(d for d in blocks if d > 1)
            if rest:
                dense.update(zip(rest, expand(sz, after([blocks[d] for d in rest], *here))))
        if i == 1:
            keep = keep_rows(sz, after([out_mask], *here)[0])
            gate.append(keep)
        keys = None
        if i == 3:
            keys = [(0, None), (1, 0), (-1, 0)]
        elif i == 4:
            keys = [(2, None), (-2, None), (1, 1), (-1, 1)]
        elif i > 4 and h == 1:
            keys = [(step, None), (-step, None)]
        if keys:
            dist = sorted(dense)
            chunks = [list(pieces[key]) for key, _ in keys]
            (chunks[0][0],) = after([chunks[0][0]], *here)
            if keys[0][0] == half - 1:
                acc = near_product(sz, acc, lefts[:2], chunks)
            else:
                then = () if lefts else (half - 1, 1 - half, half)
                acc, *more = product(sz, acc, dist, [dense[d] for d in dist], chunks, keys, then)
                lefts = lefts or more
            gate.append(acc)
        if i + 3 == len(arrivals):
            early = last_hop(after(final[:1], acc)[0], 1, 1, keep=True)
    second = [early, last_hop(after(final[1:], *here)[0], -1, 1)]
    left = lefts[2]
    mine, sums = last_product(sz, 0, acc, left, first, keep)
    other, sums = last_product(sz, 1, acc, left, second, keep, sums)
    return scale(sz, mine, other, column_sums(sz, sums))


def solution(mesh):
    placed = (P("row", "col"), P("row", "col"), P("row", "col"))
    return jax.shard_map(
        functools.partial(per_device, mesh.shape["row"], mesh.shape["col"]),
        mesh=mesh,
        in_specs=placed,
        out_specs=P("row", "col"),
        check_vma=False,
    )
```

```python
import functools

import jax
import jax.numpy as jnp
from jax import lax
from jax.experimental import pallas as pl
from jax.experimental.pallas import tpu as pltpu
from jax.sharding import PartitionSpec as P

CODE_ROWS = 16
VMEM_LIMIT = 16 * 1024 * 1024


def cost(weight=1):
    return pl.CostEstimate(flops=weight << 29, bytes_accessed=0, transcendentals=0)


class Sizes:
    def __init__(self, matrix, in_mask, n_row, n_col):
        self.rows, self.cols = matrix.shape
        self.tr, self.tc = in_mask.shape
        self.tile = self.rows // self.tr
        self.cap = self.tr * self.tc * 3 // 4
        self.wide = min(self.tile, 128)
        self.parts = self.tile // self.wide
        self.slot = self.parts * self.tile
        self.pay_rows = CODE_ROWS + self.cap * self.slot
        self.buf_rows = self.pay_rows + self.slot
        self.cut = CODE_ROWS + (self.cap + 1) // 2 * self.slot
        self.chunks = ((0, self.cut), (self.cut, self.pay_rows - self.cut))
        self.n_row, self.n_col = n_row, n_col


def ring_order(n_row):
    n_out = 4 if n_row % 4 == 0 else 2
    n_in = n_row // n_out
    ring = [(0, 0)]
    for o in range(n_out):
        inner = list(range(1, n_in))
        ring += [(o, i) for i in (inner if o % 2 == 0 else inner[::-1])]
    ring += [(o, 0) for o in range(n_out - 1, 0, -1)]
    return [o * n_in + i for o, i in ring]


def pick(values, index):
    out = jnp.int32(values[0])
    for i, value in enumerate(values[1:], 1):
        out = jnp.where(index == i, value, out)
    return out


def origin(sz, key):
    ring = ring_order(sz.n_row)
    rows = [ring[(ring.index(q) - key) % sz.n_row] for q in range(sz.n_row)]
    return pick(rows, lax.axis_index("row"))


def pack_kernel(sz, mask_ref, matrix_ref, whole_ref, *chunk_refs):
    flags = [
        (mask_ref[t // sz.tc, t % sz.tc] != 0).astype(jnp.int32) for t in range(sz.tr * sz.tc)
    ]
    before, count = [], jnp.int32(0)
    for flag in flags:
        before.append(count)
        count = count + flag
    code = jnp.int32(0)
    for t, flag in enumerate(flags):
        code = code + flag * (1 << t)
    codes = jnp.full((CODE_ROWS, sz.wide), code.astype(jnp.float32), jnp.float32)
    codes = codes.astype(jnp.bfloat16)
    whole_ref[0:CODE_ROWS, :] = codes
    chunk_refs[0][0:CODE_ROWS, :] = codes
    for s in range(sz.cap):
        which = jnp.int32(0)
        for t, flag in enumerate(flags):
            which = jnp.where((flag == 1) & (before[t] == s), t, which)
        row = pl.multiple_of(which // sz.tc * sz.tile, sz.tile)
        col = pl.multiple_of(which % sz.tc * sz.tile, sz.tile)
        values = matrix_ref[pl.ds(row, sz.tile), pl.ds(col, sz.tile)]
        for j in range(sz.parts):
            part = values[:, j * sz.wide : (j + 1) * sz.wide]
            at = CODE_ROWS + s * sz.slot + j * sz.tile
            whole_ref[at : at + sz.tile, :] = part
            for ref, (start, size) in zip(chunk_refs, sz.chunks):
                if start <= at < start + size:
                    ref[at - start : at - start + sz.tile, :] = part


def pack(sz, matrix, in_mask):
    vmem = pl.BlockSpec(memory_space=pltpu.VMEM)
    sizes = [sz.pay_rows] + [size for _, size in sz.chunks]
    return pl.pallas_call(
        functools.partial(pack_kernel, sz),
        out_shape=[pltpu.VMEM((size, sz.wide), jnp.bfloat16) for size in sizes],
        in_specs=[pl.BlockSpec(memory_space=pltpu.SMEM), vmem],
        out_specs=[vmem] * len(sizes),
        compiler_params=pltpu.CompilerParams(vmem_limit_bytes=VMEM_LIMIT),
        name="pack_tiles",
    )(*(pltpu.with_memory_space_constraint(x, pltpu.HBM) for x in (in_mask, matrix)))


def slots_of(sz, code_block):
    code = jnp.max(code_block.astype(jnp.float32)).astype(jnp.int32)
    slots, count = [], jnp.int32(0)
    for t in range(sz.tr * sz.tc):
        flag = lax.rem(lax.shift_right_logical(code, jnp.int32(t)), jnp.int32(2))
        slots.append(jnp.where(flag == 1, count, sz.cap))
        count = count + flag
    return slots


def load_tile(sz, buf, slot):
    at = CODE_ROWS + slot * sz.slot
    parts = [
        buf[pl.ds(pl.multiple_of(at + j * sz.tile, 16), sz.tile), :] for j in range(sz.parts)
    ]
    return jnp.concatenate(parts, axis=1)


def clear_spare(sz, buf):
    buf[sz.pay_rows :, :] = jnp.zeros((sz.slot, sz.wide), jnp.bfloat16)


def expand_kernel(sz, n, *refs):
    pays, dense, (buf, sems) = refs[:n], refs[n : 2 * n], refs[2 * n :]
    copies = []
    for p in range(n):
        copy = pltpu.make_async_copy(pays[p], buf.at[p, pl.ds(0, sz.pay_rows)], sems.at[p])
        copy.start()
        copies.append(copy)
        clear_spare(sz, buf.at[p])
    for p in range(n):
        copies[p].wait()
        slots = slots_of(sz, buf[p, 0:CODE_ROWS, :])
        for t in range(sz.tr * sz.tc):
            a, k = t // sz.tc, t % sz.tc
            rows, cols = slice(a * sz.tile, (a + 1) * sz.tile), slice(k * sz.tile, (k + 1) * sz.tile)
            dense[p][rows, cols] = load_tile(sz, buf.at[p], slots[t])


def expand(sz, pays, weight=1):
    n = len(pays)
    return pl.pallas_call(
        functools.partial(expand_kernel, sz, n),
        out_shape=[jax.ShapeDtypeStruct((sz.rows, sz.cols), jnp.bfloat16)] * n,
        in_specs=[pl.BlockSpec(memory_space=pltpu.HBM)] * n,
        out_specs=[pl.BlockSpec(memory_space=pltpu.VMEM)] * n,
        scratch_shapes=[
            pltpu.VMEM((n, sz.buf_rows, sz.wide), jnp.bfloat16),
            pltpu.SemaphoreType.DMA((n,)),
        ],
        compiler_params=pltpu.CompilerParams(vmem_limit_bytes=2 * VMEM_LIMIT),
        cost_estimate=cost(weight),
        name="expand_tiles",
    )(*pays)


def load_right(sz, buf, slots, b):
    tiles = [load_tile(sz, buf, slots[k * sz.tc + b]) for k in range(sz.tr)]
    return jnp.concatenate(tiles, axis=0)


def start_left(sz, dist, blocks, key, into, sem):
    row = origin(sz, key)
    per_block = sz.cols // sz.rows
    column = pl.multiple_of(lax.rem(row, per_block) * sz.rows, sz.rows)
    apart = (row // per_block) ^ lax.axis_index("col")
    for d, block in zip(dist, blocks):

        @pl.when(apart == d)
        def _():
            pltpu.make_async_copy(block.at[:, pl.ds(column, sz.rows)], into, sem).start()


def wait_left(sz, blocks, into, sem):
    pltpu.make_async_copy(blocks[0].at[:, pl.ds(0, sz.rows)], into, sem).wait()


def on_core(core):
    if core is None:
        return jnp.bool_(True)
    return lax.axis_index("col") % 2 == core


def product_kernel(sz, dist, keys, first, then, *refs):
    refs = list(refs)
    blocks = [refs.pop(0) for _ in dist]
    pays = [[refs.pop(0) for _ in sz.chunks] for _ in keys]
    before_ref = None if first else refs.pop(0)
    out_ref = refs.pop(0)
    then_refs = [refs.pop(0) for _ in then]
    buf, left, sems = refs
    per_piece = len(sz.chunks) + 1

    def copies(p):
        return [
            pltpu.make_async_copy(
                pays[p][h], buf.at[p, pl.ds(*chunk)], sems.at[p * per_piece + 1 + h]
            )
            for h, chunk in enumerate(sz.chunks)
        ]

    def begin(p, key):
        start_left(sz, dist, blocks, key, left.at[p], sems.at[p * per_piece])
        for copy in copies(p):
            copy.start()

    def add(p):
        clear_spare(sz, buf.at[p])
        wait_left(sz, blocks, left.at[p], sems.at[p * per_piece])
        for copy in copies(p):
            copy.wait()
        slots = slots_of(sz, buf[p, 0:CODE_ROWS, :])
        for b in range(sz.tc):
            cols = slice(b * sz.tile, (b + 1) * sz.tile)
            term = jnp.dot(
                left[p], load_right(sz, buf.at[p], slots, b), preferred_element_type=jnp.float32
            )
            if p:
                term = term + out_ref[:, cols]
            elif not first:
                term = term + before_ref[:, cols]
            out_ref[:, cols] = term

    for p, (key, core) in enumerate(keys):
        if core is None:
            begin(p, key)
        else:
            pl.when(on_core(core))(functools.partial(begin, p, key))
    for t, (key, ref) in enumerate(zip(then, then_refs)):
        start_left(sz, dist, blocks, key, ref, sems.at[len(keys) * per_piece + t])
    for p, (key, core) in enumerate(keys):
        if core is None:
            add(p)
        else:
            pl.when(on_core(core))(functools.partial(add, p))
    for t, ref in enumerate(then_refs):
        wait_left(sz, blocks, ref, sems.at[len(keys) * per_piece + t])


def product(sz, before, dist, blocks, pieces, keys, then=()):
    n = len(keys)
    first = before is None
    vmem = pl.BlockSpec(memory_space=pltpu.VMEM)
    chunks = [chunk for piece in pieces for chunk in piece]
    in_specs = [pl.BlockSpec(memory_space=pl.ANY)] * len(blocks)
    in_specs += [pl.BlockSpec(memory_space=pltpu.HBM)] * len(chunks)
    args = [*blocks, *chunks]
    if not first:
        in_specs.append(vmem)
        args.append(before)
    out_shape = [jax.ShapeDtypeStruct((sz.rows, sz.cols), jnp.float32)]
    out_shape += [jax.ShapeDtypeStruct((sz.rows, sz.rows), jnp.bfloat16)] * len(then)
    return pl.pallas_call(
        functools.partial(product_kernel, sz, dist, keys, first, then),
        out_shape=out_shape,
        in_specs=in_specs,
        out_specs=[vmem] * len(out_shape),
        scratch_shapes=[
            pltpu.VMEM((n, sz.buf_rows, sz.wide), jnp.bfloat16),
            pltpu.VMEM((n, sz.rows, sz.rows), jnp.bfloat16),
            pltpu.SemaphoreType.DMA((n * (len(sz.chunks) + 1) + max(1, len(then)),)),
        ],
        compiler_params=pltpu.CompilerParams(vmem_limit_bytes=VMEM_LIMIT),
        cost_estimate=cost(),
        name="product",
    )(*args)


def near_kernel(sz, n, *refs):
    refs = list(refs)
    lefts = [refs.pop(0) for _ in range(n)]
    pays = [[refs.pop(0) for _ in sz.chunks] for _ in range(n)]
    before_ref, out_ref, buf = refs
    slots = []
    for p in range(n):
        for ref, chunk in zip(pays[p], sz.chunks):
            buf[p, pl.ds(*chunk), :] = ref[...]
        clear_spare(sz, buf.at[p])
        slots.append(slots_of(sz, buf[p, 0:CODE_ROWS, :]))
    for b in range(sz.tc):
        cols = slice(b * sz.tile, (b + 1) * sz.tile)
        total = before_ref[:, cols]
        for p in range(n):
            total = total + jnp.dot(
                lefts[p][...],
                load_right(sz, buf.at[p], slots[p], b),
                preferred_element_type=jnp.float32,
            )
        out_ref[:, cols] = total


def near_product(sz, before, lefts, pieces):
    n = len(pieces)
    args = [*lefts, *(chunk for piece in pieces for chunk in piece), before]
    vmem = pl.BlockSpec(memory_space=pltpu.VMEM)
    return pl.pallas_call(
        functools.partial(near_kernel, sz, n),
        out_shape=jax.ShapeDtypeStruct((sz.rows, sz.cols), jnp.float32),
        in_specs=[vmem] * len(args),
        out_specs=vmem,
        scratch_shapes=[pltpu.VMEM((n, sz.buf_rows, sz.wide), jnp.bfloat16)],
        compiler_params=pltpu.CompilerParams(vmem_limit_bytes=VMEM_LIMIT),
        cost_estimate=cost(),
        name="product_near",
    )(*args)


def keep_kernel(sz, out_mask_ref, keep_ref):
    for a in range(sz.tr):
        for b in range(sz.tc):
            rows, cols = slice(a * 8, (a + 1) * 8), slice(b * sz.tile, (b + 1) * sz.tile)
            kept = (out_mask_ref[a, b] != 0).astype(jnp.float32)
            keep_ref[rows, cols] = jnp.full((8, sz.tile), kept, jnp.float32)


def keep_rows(sz, out_mask):
    return pl.pallas_call(
        functools.partial(keep_kernel, sz),
        out_shape=jax.ShapeDtypeStruct((8 * sz.tr, sz.cols), jnp.float32),
        in_specs=[pl.BlockSpec(memory_space=pltpu.SMEM)],
        out_specs=pl.BlockSpec(memory_space=pltpu.VMEM),
        compiler_params=pltpu.CompilerParams(vmem_limit_bytes=VMEM_LIMIT),
        cost_estimate=cost(),
        name="keep_rows",
    )(out_mask)


def last_kernel(sz, core, keep_ref, left_ref, *refs):
    refs = list(refs)
    pays = [refs.pop(0) for _ in sz.chunks]
    before_ref = refs.pop(0)
    known_ref = refs.pop(0) if core else None
    out_ref, sums_ref, buf = refs
    here = lax.axis_index("col") % 2 == core

    @pl.when(here)
    def _():
        for ref, chunk in zip(pays, sz.chunks):
            buf[pl.ds(*chunk), :] = ref[...]
        clear_spare(sz, buf)
        slots = slots_of(sz, buf[0:CODE_ROWS, :])
        for b in range(sz.tc):
            cols = slice(b * sz.tile, (b + 1) * sz.tile)
            block = before_ref[:, cols] + jnp.dot(
                left_ref[...], load_right(sz, buf, slots, b), preferred_element_type=jnp.float32
            )
            total = jnp.zeros((1, sz.tile), jnp.float32)
            for a in range(sz.tr):
                rows = slice(a * sz.tile, (a + 1) * sz.tile)
                part = block[rows]
                kept = keep_ref[a * 8 : a * 8 + 1, cols] != 0
                part = jnp.where(kept, part * part, jnp.zeros_like(part))
                out_ref[rows, cols] = part
                total = total + jnp.sum(part, axis=0, keepdims=True)
            sums_ref[:, cols] = total

    @pl.when(jnp.logical_not(here))
    def _():
        sums_ref[...] = jnp.zeros_like(sums_ref) if known_ref is None else known_ref[...]


def last_product(sz, core, before, left, piece, keep, known=None):
    vmem = pl.BlockSpec(memory_space=pltpu.VMEM)
    args = [keep, left, *piece, before] + ([] if known is None else [known])
    return pl.pallas_call(
        functools.partial(last_kernel, sz, core),
        out_shape=[
            jax.ShapeDtypeStruct((sz.rows, sz.cols), jnp.float32),
            jax.ShapeDtypeStruct((1, sz.cols), jnp.float32),
        ],
        in_specs=[vmem] * len(args),
        out_specs=[vmem] * 2,
        scratch_shapes=[pltpu.VMEM((sz.buf_rows, sz.wide), jnp.bfloat16)],
        compiler_params=pltpu.CompilerParams(vmem_limit_bytes=VMEM_LIMIT),
        cost_estimate=cost(),
        name="product_last",
    )(*args)


def scale_kernel(sz, steps, first_ref, second_ref, totals_ref, flow_ref, buf, sems):
    total_rows = float(sz.rows * sz.n_row)
    size = sz.rows // steps
    totals = totals_ref[...]
    copies = []
    for s in range(steps):
        rows = pl.ds(s * size, size)
        for core, ref in enumerate((first_ref, second_ref)):

            @pl.when(lax.axis_index("col") % 2 == core)
            def _():
                buf[rows, :] = total_rows * ref[rows, :] / totals

        copies.append(pltpu.make_async_copy(buf.at[rows], flow_ref.at[rows], sems.at[s]))
        copies[-1].start()
    for copy in copies:
        copy.wait()


def scale(sz, first, second, totals):
    vmem = pl.BlockSpec(memory_space=pltpu.VMEM)
    steps = 4
    return pl.pallas_call(
        functools.partial(scale_kernel, sz, steps),
        out_shape=jax.ShapeDtypeStruct((sz.rows, sz.cols), jnp.float32),
        in_specs=[vmem] * 3,
        out_specs=pl.BlockSpec(memory_space=pltpu.HBM),
        scratch_shapes=[
            pltpu.VMEM((sz.rows, sz.cols), jnp.float32),
            pltpu.SemaphoreType.DMA((steps,)),
        ],
        compiler_params=pltpu.CompilerParams(vmem_limit_bytes=VMEM_LIMIT),
        cost_estimate=cost(),
        name="scale",
    )(first, second, totals)


def column_sums(sz, sums):
    if sz.n_row % 2:
        return lax.psum(sums, "row")
    pair = sums + lax.ppermute(sums, "row", [(q, q ^ 1) for q in range(sz.n_row)])
    others = [
        lax.ppermute(pair, "row", [(q, (q + 2 * t) % sz.n_row) for q in range(sz.n_row)])
        for t in range(1, sz.n_row // 2)
    ]
    return functools.reduce(jnp.add, others, pair)


def after(values, *anchors):
    return lax.optimization_barrier((*values, *anchors))[: len(values)]


def per_device(n_row, n_col, matrix, in_mask, out_mask):
    sz = Sizes(matrix, in_mask, n_row, n_col)
    ring = ring_order(n_row)
    half = n_row // 2

    whole, *own = pack(sz, matrix, in_mask)

    def hop(chunk, way):
        pairs = [(ring[p], ring[(p + way) % n_row]) for p in range(n_row)]
        return lax.ppermute(chunk, "row", pairs)

    def last_hop(chunk, way, core, keep=False):
        aside = 2 if n_col % 4 == 0 and not keep else 0
        pairs = []
        for p in range(n_row):
            for c in range(n_col):
                mine = c % 2 == core
                to = (ring[(p + way) % n_row], c) if mine else (ring[p], c ^ aside)
                pairs.append((ring[p] * n_col + c, to[0] * n_col + to[1]))
        return lax.ppermute(chunk, ("row", "col"), pairs)

    def apart(value, far):
        return lax.ppermute(value, "col", [(q, q ^ far) for q in range(n_col)])

    lead = {1: 0, -1: 1}
    pieces = {0: list(own)}
    arrivals = [(step, h) for step in range(1, half + 1) for h in (0, 1)][:-1]

    def send(step, h, sources):
        key = {way: way * step if step < half else half for way in (1, -1)}
        for way, source in zip((1, -1), sources):
            pieces.setdefault(key[way], [None] * 2)[lead[way] ^ h] = hop(source, way)

    def arrived(step, h):
        return [pieces[way * step if step < half else half][lead[way] ^ h] for way in (1, -1)]

    for h in (0, 1):
        send(1, h, [own[lead[way] ^ h] for way in (1, -1)])
    far = n_col // 2
    blocks, dense = {0: whole, 1: apart(whole, 1)}, {}
    acc, lefts, gate = None, [], []
    for i, (step, h) in enumerate(arrivals[:-1]):
        here = after(arrived(step, h), *gate)
        if i + 3 < len(arrivals):
            send(step + 1, h, here)
        elif i + 2 < len(arrivals):
            final = list(here)
            first = [last_hop(chunk, way, 0) for chunk, way in zip(final, (1, -1))]
        gate = list(here)
        if i == 0:
            mine, near = after([blocks[0], blocks[1]], *here)
            (dense[0],) = expand(sz, [mine], 12)
            if far > 1:
                blocks[far] = apart(after([whole], blocks[1])[0], far)
            gate += [dense[0], near]
        if i == 1:
            (dense[1],) = expand(sz, after([blocks[1]], *here), 12)
            gate += [dense[1]]
        if i == 1 and far > 1:
            (blocks[far],) = after([blocks[far]], *here)
        if i == 3:
            bit = far
            while bit > 2:
                bit //= 2
                for d in [d for d in blocks if d != 1]:
                    blocks[d ^ bit] = apart(blocks[d], bit)
            for d in [d for d in blocks if d > 1]:
                blocks[d ^ 1] = apart(blocks[d], 1)
            rest = sorted(d for d in blocks if d > 1)
            if rest:
                dense.update(zip(rest, expand(sz, after([blocks[d] for d in rest], *here))))
        if i == 1:
            keep = keep_rows(sz, after([out_mask], *here)[0])
            gate.append(keep)
        keys = None
        if i == 3:
            keys = [(0, None), (1, None), (-1, 0)]
        elif i == 4:
            keys = [(2, None), (-2, None), (-1, 1)]
        elif i > 4 and h == 1:
            keys = [(step, None), (-step, None)]
        if keys:
            dist = sorted(dense)
            chunks = [list(pieces[key]) for key, _ in keys]
            (chunks[0][0],) = after([chunks[0][0]], *here)
            if keys[0][0] == half - 1:
                acc = near_product(sz, acc, lefts[:2], chunks)
            else:
                then = () if lefts else (half - 1, 1 - half, half)
                acc, *more = product(sz, acc, dist, [dense[d] for d in dist], chunks, keys, then)
                lefts = lefts or more
            gate.append(acc)
        if i + 3 == len(arrivals):
            final = after(final, acc)
            second = [last_hop(chunk, way, 1, keep=True) for chunk, way in zip(final, (1, -1))]
    left = lefts[2]
    mine, sums = last_product(sz, 0, acc, left, first, keep)
    other, sums = last_product(sz, 1, acc, left, second, keep, sums)
    return scale(sz, mine, other, column_sums(sz, sums))


def solution(mesh):
    placed = (P("row", "col"), P("row", "col"), P("row", "col"))
    return jax.shard_map(
        functools.partial(per_device, mesh.shape["row"], mesh.shape["col"]),
        mesh=mesh,
        in_specs=placed,
        out_specs=P("row", "col"),
        check_vma=False,
    )
```

```python
import functools

import jax
import jax.numpy as jnp
from jax import lax
from jax.experimental import pallas as pl
from jax.experimental.pallas import tpu as pltpu
from jax.sharding import PartitionSpec as P

CODE_ROWS = 16
VMEM_LIMIT = 16 * 1024 * 1024


def cost(weight=1):
    return pl.CostEstimate(flops=weight << 29, bytes_accessed=0, transcendentals=0)


class Sizes:
    def __init__(self, matrix, in_mask, n_row, n_col):
        self.rows, self.cols = matrix.shape
        self.tr, self.tc = in_mask.shape
        self.tile = self.rows // self.tr
        self.cap = self.tr * self.tc * 3 // 4
        self.wide = min(self.tile, 128)
        self.parts = self.tile // self.wide
        self.slot = self.parts * self.tile
        self.pay_rows = CODE_ROWS + self.cap * self.slot
        self.buf_rows = self.pay_rows + self.slot
        self.cut = CODE_ROWS + (self.cap + 1) // 2 * self.slot
        self.chunks = ((0, self.cut), (self.cut, self.pay_rows - self.cut))
        self.n_row, self.n_col = n_row, n_col


def ring_order(n_row):
    n_out = 4 if n_row % 4 == 0 else 2
    n_in = n_row // n_out
    ring = [(0, 0)]
    for o in range(n_out):
        inner = list(range(1, n_in))
        ring += [(o, i) for i in (inner if o % 2 == 0 else inner[::-1])]
    ring += [(o, 0) for o in range(n_out - 1, 0, -1)]
    return [o * n_in + i for o, i in ring]


def pick(values, index):
    out = jnp.int32(values[0])
    for i, value in enumerate(values[1:], 1):
        out = jnp.where(index == i, value, out)
    return out


def origin(sz, key):
    ring = ring_order(sz.n_row)
    rows = [ring[(ring.index(q) - key) % sz.n_row] for q in range(sz.n_row)]
    return pick(rows, lax.axis_index("row"))


def pack_kernel(sz, mask_ref, matrix_ref, whole_ref, *chunk_refs):
    flags = [
        (mask_ref[t // sz.tc, t % sz.tc] != 0).astype(jnp.int32) for t in range(sz.tr * sz.tc)
    ]
    before, count = [], jnp.int32(0)
    for flag in flags:
        before.append(count)
        count = count + flag
    code = jnp.int32(0)
    for t, flag in enumerate(flags):
        code = code + flag * (1 << t)
    codes = jnp.full((CODE_ROWS, sz.wide), code.astype(jnp.float32), jnp.float32)
    codes = codes.astype(jnp.bfloat16)
    whole_ref[0:CODE_ROWS, :] = codes
    chunk_refs[0][0:CODE_ROWS, :] = codes
    for s in range(sz.cap):
        which = jnp.int32(0)
        for t, flag in enumerate(flags):
            which = jnp.where((flag == 1) & (before[t] == s), t, which)
        row = pl.multiple_of(which // sz.tc * sz.tile, sz.tile)
        col = pl.multiple_of(which % sz.tc * sz.tile, sz.tile)
        values = matrix_ref[pl.ds(row, sz.tile), pl.ds(col, sz.tile)]
        for j in range(sz.parts):
            part = values[:, j * sz.wide : (j + 1) * sz.wide]
            at = CODE_ROWS + s * sz.slot + j * sz.tile
            whole_ref[at : at + sz.tile, :] = part
            for ref, (start, size) in zip(chunk_refs, sz.chunks):
                if start <= at < start + size:
                    ref[at - start : at - start + sz.tile, :] = part


def pack(sz, matrix, in_mask):
    vmem = pl.BlockSpec(memory_space=pltpu.VMEM)
    sizes = [sz.pay_rows] + [size for _, size in sz.chunks]
    return pl.pallas_call(
        functools.partial(pack_kernel, sz),
        out_shape=[pltpu.VMEM((size, sz.wide), jnp.bfloat16) for size in sizes],
        in_specs=[pl.BlockSpec(memory_space=pltpu.SMEM), vmem],
        out_specs=[vmem] * len(sizes),
        compiler_params=pltpu.CompilerParams(vmem_limit_bytes=VMEM_LIMIT),
        name="pack_tiles",
    )(*(pltpu.with_memory_space_constraint(x, pltpu.HBM) for x in (in_mask, matrix)))


def slots_of(sz, code_block):
    code = jnp.max(code_block.astype(jnp.float32)).astype(jnp.int32)
    slots, count = [], jnp.int32(0)
    for t in range(sz.tr * sz.tc):
        flag = lax.rem(lax.shift_right_logical(code, jnp.int32(t)), jnp.int32(2))
        slots.append(jnp.where(flag == 1, count, sz.cap))
        count = count + flag
    return slots


def load_tile(sz, buf, slot):
    at = CODE_ROWS + slot * sz.slot
    parts = [
        buf[pl.ds(pl.multiple_of(at + j * sz.tile, 16), sz.tile), :] for j in range(sz.parts)
    ]
    return jnp.concatenate(parts, axis=1)


def clear_spare(sz, buf):
    buf[sz.pay_rows :, :] = jnp.zeros((sz.slot, sz.wide), jnp.bfloat16)


def expand_kernel(sz, n, *refs):
    pays, dense, (buf, sems) = refs[:n], refs[n : 2 * n], refs[2 * n :]
    copies = []
    for p in range(n):
        copy = pltpu.make_async_copy(pays[p], buf.at[p, pl.ds(0, sz.pay_rows)], sems.at[p])
        copy.start()
        copies.append(copy)
        clear_spare(sz, buf.at[p])
    for p in range(n):
        copies[p].wait()
        slots = slots_of(sz, buf[p, 0:CODE_ROWS, :])
        for t in range(sz.tr * sz.tc):
            a, k = t // sz.tc, t % sz.tc
            rows, cols = slice(a * sz.tile, (a + 1) * sz.tile), slice(k * sz.tile, (k + 1) * sz.tile)
            dense[p][rows, cols] = load_tile(sz, buf.at[p], slots[t])


def expand(sz, pays, weight=1):
    n = len(pays)
    return pl.pallas_call(
        functools.partial(expand_kernel, sz, n),
        out_shape=[jax.ShapeDtypeStruct((sz.rows, sz.cols), jnp.bfloat16)] * n,
        in_specs=[pl.BlockSpec(memory_space=pltpu.HBM)] * n,
        out_specs=[pl.BlockSpec(memory_space=pltpu.VMEM)] * n,
        scratch_shapes=[
            pltpu.VMEM((n, sz.buf_rows, sz.wide), jnp.bfloat16),
            pltpu.SemaphoreType.DMA((n,)),
        ],
        compiler_params=pltpu.CompilerParams(vmem_limit_bytes=2 * VMEM_LIMIT),
        cost_estimate=cost(weight),
        name="expand_tiles",
    )(*pays)


def load_right(sz, buf, slots, b):
    tiles = [load_tile(sz, buf, slots[k * sz.tc + b]) for k in range(sz.tr)]
    return jnp.concatenate(tiles, axis=0)


def start_left(sz, dist, blocks, key, into, sem):
    row = origin(sz, key)
    per_block = sz.cols // sz.rows
    column = pl.multiple_of(lax.rem(row, per_block) * sz.rows, sz.rows)
    apart = (row // per_block) ^ lax.axis_index("col")
    for d, block in zip(dist, blocks):

        @pl.when(apart == d)
        def _():
            pltpu.make_async_copy(block.at[:, pl.ds(column, sz.rows)], into, sem).start()


def wait_left(sz, blocks, into, sem):
    pltpu.make_async_copy(blocks[0].at[:, pl.ds(0, sz.rows)], into, sem).wait()


def on_core(core):
    if core is None:
        return jnp.bool_(True)
    return lax.axis_index("col") % 2 == core


def product_kernel(sz, dist, keys, first, then, *refs):
    refs = list(refs)
    blocks = [refs.pop(0) for _ in dist]
    pays = [[refs.pop(0) for _ in sz.chunks] for _ in keys]
    before_ref = None if first else refs.pop(0)
    out_ref = refs.pop(0)
    then_refs = [refs.pop(0) for _ in then]
    buf, left, sems = refs
    per_piece = len(sz.chunks) + 1

    def copies(p):
        return [
            pltpu.make_async_copy(
                pays[p][h], buf.at[p, pl.ds(*chunk)], sems.at[p * per_piece + 1 + h]
            )
            for h, chunk in enumerate(sz.chunks)
        ]

    def begin(p, key):
        start_left(sz, dist, blocks, key, left.at[p], sems.at[p * per_piece])
        for copy in copies(p):
            copy.start()

    def add(p):
        clear_spare(sz, buf.at[p])
        wait_left(sz, blocks, left.at[p], sems.at[p * per_piece])
        for copy in copies(p):
            copy.wait()
        slots = slots_of(sz, buf[p, 0:CODE_ROWS, :])
        for b in range(sz.tc):
            cols = slice(b * sz.tile, (b + 1) * sz.tile)
            term = jnp.dot(
                left[p], load_right(sz, buf.at[p], slots, b), preferred_element_type=jnp.float32
            )
            if p:
                term = term + out_ref[:, cols]
            elif not first:
                term = term + before_ref[:, cols]
            out_ref[:, cols] = term

    for p, (key, core) in enumerate(keys):
        if core is None:
            begin(p, key)
        else:
            pl.when(on_core(core))(functools.partial(begin, p, key))
    for t, (key, ref) in enumerate(zip(then, then_refs)):
        start_left(sz, dist, blocks, key, ref, sems.at[len(keys) * per_piece + t])
    for p, (key, core) in enumerate(keys):
        if core is None:
            add(p)
        else:
            pl.when(on_core(core))(functools.partial(add, p))
    for t, ref in enumerate(then_refs):
        wait_left(sz, blocks, ref, sems.at[len(keys) * per_piece + t])


def product(sz, before, dist, blocks, pieces, keys, then=()):
    n = len(keys)
    first = before is None
    vmem = pl.BlockSpec(memory_space=pltpu.VMEM)
    chunks = [chunk for piece in pieces for chunk in piece]
    in_specs = [pl.BlockSpec(memory_space=pl.ANY)] * len(blocks)
    in_specs += [pl.BlockSpec(memory_space=pltpu.HBM)] * len(chunks)
    args = [*blocks, *chunks]
    if not first:
        in_specs.append(vmem)
        args.append(before)
    out_shape = [jax.ShapeDtypeStruct((sz.rows, sz.cols), jnp.float32)]
    out_shape += [jax.ShapeDtypeStruct((sz.rows, sz.rows), jnp.bfloat16)] * len(then)
    return pl.pallas_call(
        functools.partial(product_kernel, sz, dist, keys, first, then),
        out_shape=out_shape,
        in_specs=in_specs,
        out_specs=[vmem] * len(out_shape),
        scratch_shapes=[
            pltpu.VMEM((n, sz.buf_rows, sz.wide), jnp.bfloat16),
            pltpu.VMEM((n, sz.rows, sz.rows), jnp.bfloat16),
            pltpu.SemaphoreType.DMA((n * (len(sz.chunks) + 1) + max(1, len(then)),)),
        ],
        compiler_params=pltpu.CompilerParams(vmem_limit_bytes=VMEM_LIMIT),
        cost_estimate=cost(),
        name="product",
    )(*args)


def near_kernel(sz, n, *refs):
    refs = list(refs)
    lefts = [refs.pop(0) for _ in range(n)]
    pays = [[refs.pop(0) for _ in sz.chunks] for _ in range(n)]
    before_ref, out_ref, buf = refs
    slots = []
    for p in range(n):
        for ref, chunk in zip(pays[p], sz.chunks):
            buf[p, pl.ds(*chunk), :] = ref[...]
        clear_spare(sz, buf.at[p])
        slots.append(slots_of(sz, buf[p, 0:CODE_ROWS, :]))
    for b in range(sz.tc):
        cols = slice(b * sz.tile, (b + 1) * sz.tile)
        total = before_ref[:, cols]
        for p in range(n):
            total = total + jnp.dot(
                lefts[p][...],
                load_right(sz, buf.at[p], slots[p], b),
                preferred_element_type=jnp.float32,
            )
        out_ref[:, cols] = total


def near_product(sz, before, lefts, pieces):
    n = len(pieces)
    args = [*lefts, *(chunk for piece in pieces for chunk in piece), before]
    vmem = pl.BlockSpec(memory_space=pltpu.VMEM)
    return pl.pallas_call(
        functools.partial(near_kernel, sz, n),
        out_shape=jax.ShapeDtypeStruct((sz.rows, sz.cols), jnp.float32),
        in_specs=[vmem] * len(args),
        out_specs=vmem,
        scratch_shapes=[pltpu.VMEM((n, sz.buf_rows, sz.wide), jnp.bfloat16)],
        compiler_params=pltpu.CompilerParams(vmem_limit_bytes=VMEM_LIMIT),
        cost_estimate=cost(),
        name="product_near",
    )(*args)


def keep_kernel(sz, out_mask_ref, keep_ref):
    for a in range(sz.tr):
        for b in range(sz.tc):
            rows, cols = slice(a * 8, (a + 1) * 8), slice(b * sz.tile, (b + 1) * sz.tile)
            kept = (out_mask_ref[a, b] != 0).astype(jnp.float32)
            keep_ref[rows, cols] = jnp.full((8, sz.tile), kept, jnp.float32)


def keep_rows(sz, out_mask):
    return pl.pallas_call(
        functools.partial(keep_kernel, sz),
        out_shape=jax.ShapeDtypeStruct((8 * sz.tr, sz.cols), jnp.float32),
        in_specs=[pl.BlockSpec(memory_space=pltpu.SMEM)],
        out_specs=pl.BlockSpec(memory_space=pltpu.VMEM),
        compiler_params=pltpu.CompilerParams(vmem_limit_bytes=VMEM_LIMIT),
        cost_estimate=cost(),
        name="keep_rows",
    )(out_mask)


def last_kernel(sz, core, keep_ref, left_ref, *refs):
    refs = list(refs)
    pays = [refs.pop(0) for _ in sz.chunks]
    before_ref = refs.pop(0)
    known_ref = refs.pop(0) if core else None
    out_ref, sums_ref, buf = refs
    here = lax.axis_index("col") % 2 == core

    @pl.when(here)
    def _():
        for ref, chunk in zip(pays, sz.chunks):
            buf[pl.ds(*chunk), :] = ref[...]
        clear_spare(sz, buf)
        slots = slots_of(sz, buf[0:CODE_ROWS, :])
        for b in range(sz.tc):
            cols = slice(b * sz.tile, (b + 1) * sz.tile)
            block = before_ref[:, cols] + jnp.dot(
                left_ref[...], load_right(sz, buf, slots, b), preferred_element_type=jnp.float32
            )
            total = jnp.zeros((1, sz.tile), jnp.float32)
            for a in range(sz.tr):
                rows = slice(a * sz.tile, (a + 1) * sz.tile)
                part = block[rows]
                kept = keep_ref[a * 8 : a * 8 + 1, cols] != 0
                part = jnp.where(kept, part * part, jnp.zeros_like(part))
                out_ref[rows, cols] = part
                total = total + jnp.sum(part, axis=0, keepdims=True)
            sums_ref[:, cols] = total

    @pl.when(jnp.logical_not(here))
    def _():
        sums_ref[...] = jnp.zeros_like(sums_ref) if known_ref is None else known_ref[...]


def last_product(sz, core, before, left, piece, keep, known=None):
    vmem = pl.BlockSpec(memory_space=pltpu.VMEM)
    args = [keep, left, *piece, before] + ([] if known is None else [known])
    return pl.pallas_call(
        functools.partial(last_kernel, sz, core),
        out_shape=[
            jax.ShapeDtypeStruct((sz.rows, sz.cols), jnp.float32),
            jax.ShapeDtypeStruct((1, sz.cols), jnp.float32),
        ],
        in_specs=[vmem] * len(args),
        out_specs=[vmem] * 2,
        scratch_shapes=[pltpu.VMEM((sz.buf_rows, sz.wide), jnp.bfloat16)],
        compiler_params=pltpu.CompilerParams(vmem_limit_bytes=VMEM_LIMIT),
        cost_estimate=cost(),
        name="product_last",
    )(*args)


def scale_kernel(sz, steps, first_ref, second_ref, totals_ref, flow_ref, buf, sems):
    total_rows = float(sz.rows * sz.n_row)
    size = sz.rows // steps
    totals = totals_ref[...]
    copies = []
    for s in range(steps):
        rows = pl.ds(s * size, size)
        for core, ref in enumerate((first_ref, second_ref)):

            @pl.when(lax.axis_index("col") % 2 == core)
            def _():
                buf[rows, :] = total_rows * ref[rows, :] / totals

        copies.append(pltpu.make_async_copy(buf.at[rows], flow_ref.at[rows], sems.at[s]))
        copies[-1].start()
    for copy in copies:
        copy.wait()


def scale(sz, first, second, totals):
    vmem = pl.BlockSpec(memory_space=pltpu.VMEM)
    steps = 8
    return pl.pallas_call(
        functools.partial(scale_kernel, sz, steps),
        out_shape=jax.ShapeDtypeStruct((sz.rows, sz.cols), jnp.float32),
        in_specs=[vmem] * 3,
        out_specs=pl.BlockSpec(memory_space=pltpu.HBM),
        scratch_shapes=[
            pltpu.VMEM((sz.rows, sz.cols), jnp.float32),
            pltpu.SemaphoreType.DMA((steps,)),
        ],
        compiler_params=pltpu.CompilerParams(vmem_limit_bytes=VMEM_LIMIT),
        cost_estimate=cost(),
        name="scale",
    )(first, second, totals)


def column_sums(sz, sums):
    if sz.n_row % 2:
        return lax.psum(sums, "row")
    pair = sums + lax.ppermute(sums, "row", [(q, q ^ 1) for q in range(sz.n_row)])
    others = [
        lax.ppermute(pair, "row", [(q, (q + 2 * t) % sz.n_row) for q in range(sz.n_row)])
        for t in range(1, sz.n_row // 2)
    ]
    return functools.reduce(jnp.add, others, pair)


def after(values, *anchors):
    return lax.optimization_barrier((*values, *anchors))[: len(values)]


def per_device(n_row, n_col, matrix, in_mask, out_mask):
    sz = Sizes(matrix, in_mask, n_row, n_col)
    ring = ring_order(n_row)
    half = n_row // 2

    whole, *own = pack(sz, matrix, in_mask)

    def hop(chunk, way):
        pairs = [(ring[p], ring[(p + way) % n_row]) for p in range(n_row)]
        return lax.ppermute(chunk, "row", pairs)

    def last_hop(chunk, way, core, keep=False):
        aside = 2 if n_col % 4 == 0 and not keep else 0
        pairs = []
        for p in range(n_row):
            for c in range(n_col):
                mine = c % 2 == core
                to = (ring[(p + way) % n_row], c) if mine else (ring[p], c ^ aside)
                pairs.append((ring[p] * n_col + c, to[0] * n_col + to[1]))
        return lax.ppermute(chunk, ("row", "col"), pairs)

    def apart(value, far):
        return lax.ppermute(value, "col", [(q, q ^ far) for q in range(n_col)])

    lead = {1: 0, -1: 1}
    pieces = {0: list(own)}
    arrivals = [(step, h) for step in range(1, half + 1) for h in (0, 1)][:-1]

    def send(step, h, sources):
        key = {way: way * step if step < half else half for way in (1, -1)}
        for way, source in zip((1, -1), sources):
            pieces.setdefault(key[way], [None] * 2)[lead[way] ^ h] = hop(source, way)

    def arrived(step, h):
        return [pieces[way * step if step < half else half][lead[way] ^ h] for way in (1, -1)]

    for h in (0, 1):
        send(1, h, [own[lead[way] ^ h] for way in (1, -1)])
    far = n_col // 2
    blocks, dense = {0: whole, 1: apart(whole, 1)}, {}
    acc, lefts, gate = None, [], []
    for i, (step, h) in enumerate(arrivals[:-1]):
        here = after(arrived(step, h), *gate)
        if i + 3 < len(arrivals):
            send(step + 1, h, here)
        elif i + 2 < len(arrivals):
            final = list(here)
            first = [last_hop(chunk, way, 0) for chunk, way in zip(final, (1, -1))]
        gate = list(here)
        if i == 0:
            mine, near = after([blocks[0], blocks[1]], *here)
            (dense[0],) = expand(sz, [mine], 12)
            if far > 1:
                blocks[far] = apart(after([whole], blocks[1])[0], far)
            gate += [dense[0], near]
        if i == 1:
            (dense[1],) = expand(sz, after([blocks[1]], *here), 12)
            gate += [dense[1]]
        if i == 1 and far > 1:
            (blocks[far],) = after([blocks[far]], *here)
        if i == 3:
            bit = far
            while bit > 2:
                bit //= 2
                for d in [d for d in blocks if d != 1]:
                    blocks[d ^ bit] = apart(blocks[d], bit)
            for d in [d for d in blocks if d > 1]:
                blocks[d ^ 1] = apart(blocks[d], 1)
            rest = sorted(d for d in blocks if d > 1)
            if rest:
                dense.update(zip(rest, expand(sz, after([blocks[d] for d in rest], *here))))
        if i == 1:
            keep = keep_rows(sz, after([out_mask], *here)[0])
            gate.append(keep)
        keys = None
        if i == 3:
            keys = [(0, None), (1, 0), (-1, 0)]
        elif i == 4:
            keys = [(2, None), (-2, None), (1, 1), (-1, 1)]
        elif i > 4 and h == 1:
            keys = [(step, None), (-step, None)]
        if keys:
            dist = sorted(dense)
            chunks = [list(pieces[key]) for key, _ in keys]
            (chunks[0][0],) = after([chunks[0][0]], *here)
            if keys[0][0] == half - 1:
                acc = near_product(sz, acc, lefts[:2], chunks)
            else:
                then = () if lefts else (half - 1, 1 - half, half)
                acc, *more = product(sz, acc, dist, [dense[d] for d in dist], chunks, keys, then)
                lefts = lefts or more
            gate.append(acc)
        if i + 3 == len(arrivals):
            final = after(final, acc)
            second = [last_hop(chunk, way, 1, keep=True) for chunk, way in zip(final, (1, -1))]
    left = lefts[2]
    mine, sums = last_product(sz, 0, acc, left, first, keep)
    other, sums = last_product(sz, 1, acc, left, second, keep, sums)
    return scale(sz, mine, other, column_sums(sz, sums))


def solution(mesh):
    placed = (P("row", "col"), P("row", "col"), P("row", "col"))
    return jax.shard_map(
        functools.partial(per_device, mesh.shape["row"], mesh.shape["col"]),
        mesh=mesh,
        in_specs=placed,
        out_specs=P("row", "col"),
        check_vma=False,
    )
```
